256 devices in a mesh: row: 4 (over y), col: 16 (over z, core), layer: 4 (over x).
Axes of the slice: x: 4, y: 4, z: 8, core: 2. Of those that a mesh axis runs over, the one named last changes fastest.
Arguments:
- matrix: float32 [8192, 8192], P('row', ('layer', 'col')), may hold values from -1 to 1, as said below
- pattern: int32 [64, 64], P('row', ('layer', 'col')), may hold values from 0 to 1, as said below
Outputs:
- product: float32 [8192, 8192], P('row', ('col', 'layer'))
The draws below stay inside these ranges and needn't reach their ends.
Inputs may be any that keep to these rules, and one draw needn't show every extreme that they name: symmetric: matrix[a, b] equals matrix[b, a]. `pattern`: symmetric; in each of the 4 aligned bands of 16 block columns every block row holds exactly 7 ones, and every diagonal entry is 1.
All inputs are finite; a program needn't handle non-finite values.
Results may differ from the reference program's by a relative error of at most 0.00007.
Values sent between devices are 32-bit elements; how exact they have to be, the bound alone decides.
A program may use at most 128 MiB of HBM per device.

```python
import math
import jax
import jax.numpy as jnp
from jax import lax

BS = 128
NB = 64
BANDS = 4
PER_BAND = 7


def draw_matrix(key, part):
    key = jax.random.fold_in(key, 1)
    full_order = NB * BS
    entry_scale = 1.0 / math.sqrt(2.0 * BANDS * PER_BAND * BS)
    normal_part = jax.random.normal(key, (full_order, full_order), jnp.float32)
    symmetric = normal_part + normal_part.T
    return symmetric * entry_scale


def draw_pattern(key, part):
    key = jax.random.fold_in(key, 2)
    band_width = NB // BANDS
    half_count = (PER_BAND - 1) // 2
    orders = [jax.random.permutation(jax.random.fold_in(key, 100 + band), band_width) for band in range(BANDS)]
    position = jnp.concatenate(orders).astype(jnp.int32)
    steps_pool = jnp.arange(1, (band_width - 1) // 2 + 1, dtype=jnp.int32)
    table_rows = []
    for first in range(BANDS):
        table_line = []
        for second in range(BANDS):
            if first == second:
                chosen = jax.random.permutation(jax.random.fold_in(key, 200 + first), steps_pool)[:half_count]
                offsets = jnp.concatenate([jnp.zeros((1,), jnp.int32), chosen, band_width - chosen])
            elif first < second:
                offsets = jax.random.permutation(jax.random.fold_in(key, 300 + first * BANDS + second), band_width)[:PER_BAND].astype(jnp.int32)
            else:
                mirrored = jax.random.permutation(jax.random.fold_in(key, 300 + second * BANDS + first), band_width)[:PER_BAND].astype(jnp.int32)
                offsets = (band_width - mirrored) % band_width
            table_line.append(offsets.astype(jnp.int32))
        table_rows.append(jnp.stack(table_line))
    table = jnp.stack(table_rows)
    band_of = jnp.arange(NB, dtype=jnp.int32) // band_width
    differ = (position[None, :] - position[:, None]) % band_width
    allowed = table[band_of[:, None], band_of[None, :]]
    return jnp.any(differ[:, :, None] == allowed, axis=2).astype(jnp.int32)


def setup_inputs(seed: int = 0) -> dict:
    key_of = jax.random.split(jax.random.key(seed), 3)
    matrix = draw_matrix(jax.random.fold_in(key_of[2], 71), 0)
    pattern = draw_pattern(jax.random.fold_in(key_of[2], 71), 0)
    return {"matrix": matrix, "pattern": pattern}


def reference(matrix, pattern):
    occupied_flag = pattern.astype(jnp.float32)
    blocks = matrix.reshape(NB, BS, NB, BS) * occupied_flag[:, None, :, None]
    occupied = blocks.reshape(NB * BS, NB * BS)
    return jnp.dot(occupied, occupied, precision=lax.Precision.HIGHEST, preferred_element_type=jnp.float32)
```

```python
import functools

import jax
import jax.numpy as jnp
from jax import lax
from jax.experimental import pallas as pl
from jax.experimental.pallas import tpu as pltpu
from jax.sharding import PartitionSpec as P

BS = 128
PER = 7
BAND = 16
UNITS = 8
LIST, SLOT, FLAG = 0, 1, 2


def index_tile(pattern):
    flags = pattern[:, 0]
    place = lax.broadcasted_iota(jnp.int32, (BAND, BAND), 0)
    upto = lax.broadcasted_iota(jnp.int32, (BAND, BAND), 1)
    count = jnp.sum(jnp.where(place <= upto, flags[:, None], 0), axis=0)
    order = lax.broadcasted_iota(jnp.int32, (BAND, BAND), 1)
    listed = jnp.sum((count[:, None] <= order).astype(jnp.int32), axis=0)
    rows = jnp.stack([jnp.minimum(listed, BAND - 1), jnp.clip(count - 1, 0, PER - 1), flags])
    return jnp.pad(rows, ((0, 8 - 3), (0, 128 - BAND)))


def split(value):
    high = value.astype(jnp.bfloat16)
    low = (value - high.astype(jnp.float32)).astype(jnp.bfloat16)
    return jnp.concatenate([high, low], axis=1)


def kernel(
    mat, meta_s, meta_v, out,
    packed_a, packed_b, a_units, a_meta, a_idx, b_meta, b_idx, b_dense, weights,
    partial, merged, opposite, from_left, from_right, from_twin,
    a_send, a_recv, am_send, am_recv, b_send, b_recv, bm_send, bm_recv, idx_sem,
    opp_send, opp_recv, mg_send, un_send, left_recv, right_recv, twin_send, twin_recv,
    *b_units,
):
    y, col, x = lax.axis_index("row"), lax.axis_index("col"), lax.axis_index("layer")
    z, q = col // 2, col % 2
    turn = 1 - 2 * q

    def at(row=None, col_=None, layer=None):
        return {
            "row": y if row is None else row,
            "col": col if col_ is None else col_,
            "layer": x if layer is None else layer,
        }

    def zdev(step):
        return at(col_=2 * ((z + step + 8) % 8) + q)

    def ydev(step):
        return at(row=(y + step + 4) % 4)

    def xdev(step, core):
        return at(col_=2 * z + core, layer=(x + step + 4) % 4)

    twin = at(col_=2 * z + 1 - q)
    a_partner = at(row=x, layer=y)
    a_self = x == y
    b_target = at(row=(col % 8) // 2, col_=2 * (2 * x + col // 8) + col % 2, layer=y)
    b_source = at(row=x, col_=8 * (z % 2) + 2 * y + q, layer=z // 2)
    b_self = (y == x) & ((col % 8) // 2 == y) & (2 * (2 * x + col // 8) + col % 2 == col)

    barrier = pltpu.get_barrier_semaphore()

    def greet(device):
        pl.semaphore_signal(barrier, inc=1, device_id=device, device_id_type=pl.DeviceIdType.MESH)

    for device in (
        zdev(1), zdev(-1), ydev(1), ydev(-1), twin,
        xdev(1, 0), xdev(1, 1), xdev(-1, 0), xdev(-1, 1),
    ):
        greet(device)

    @pl.when(jnp.logical_not(a_self))
    def _():
        greet(a_partner)

    @pl.when(jnp.logical_not(b_self))
    def _():
        greet(b_source)

    for s in range(PER):
        block = mat[meta_s[LIST, s]]
        packed_a[s] = block
        packed_b[s] = block.T

    expected = 11 - a_self.astype(jnp.int32) - b_self.astype(jnp.int32)
    pl.semaphore_wait(barrier, expected)

    def remote(src, dst, send, recv, device):
        return pltpu.make_async_remote_copy(
            src_ref=src, dst_ref=dst, send_sem=send, recv_sem=recv,
            device_id=device, device_id_type=pl.DeviceIdType.MESH,
        )

    def got(dst, send, recv):
        remote(dst, dst, send, recv, twin).wait_recv()

    def sent(src, send, recv):
        remote(src, src, send, recv, twin).wait_send()

    def send_a(t, data, meta, device):
        remote(meta, a_meta.at[t], am_send.at[t], am_recv.at[t], device).start()
        remote(data, a_units.at[t], a_send.at[t], a_recv.at[t], device).start()

    def send_b(u, data, meta, device):
        remote(meta, b_meta.at[u], bm_send.at[u], bm_recv.at[u], device).start()
        remote(data, b_units[u], b_send.at[u], b_recv.at[u], device).start()

    @pl.when(jnp.logical_not(b_self))
    def _():
        send_b(0, packed_b, meta_v, b_target)

    @pl.when(b_self)
    def _():
        pltpu.make_async_copy(meta_v, b_meta.at[0], bm_recv.at[0]).start()
        pltpu.make_async_copy(packed_b, b_units[0], b_recv.at[0]).start()

    @pl.when(jnp.logical_not(a_self))
    def _():
        send_a(0, packed_a, meta_v, a_partner)

    @pl.when(a_self)
    def _():
        pltpu.make_async_copy(meta_v, a_meta.at[0], am_recv.at[0]).start()
        pltpu.make_async_copy(packed_a, a_units.at[0], a_recv.at[0]).start()

    def a_arrive(t):
        got(a_meta.at[t], am_send.at[t], am_recv.at[t])
        index = pltpu.make_async_copy(a_meta.at[t], a_idx.at[t], idx_sem)
        index.start()
        got(a_units.at[t], a_send.at[t], a_recv.at[t])
        index.wait()

    def a_forward(t):
        way = jnp.where(t % 2 == 1, turn, -turn)
        send_a(t + 2, a_units.at[t], a_meta.at[t], zdev(way))

    def b_arrive(u):
        got(b_meta.at[u], bm_send.at[u], bm_recv.at[u])
        index = pltpu.make_async_copy(b_meta.at[u], b_idx.at[u], idx_sem)
        index.start()
        got(b_units[u], b_send.at[u], b_recv.at[u])
        index.wait()

    def b_unpack(u):
        way, core = (turn, q) if u < 4 else (-turn, 1 - q)
        unit = 2 * ((y + way * (0, -1, 1, -2)[u % 4] + 4) % 4) + core
        group, half = unit % 4, unit // 4

        def place(j, carry):
            block = b_units[u][b_idx[u, SLOT, j]] * b_idx[u, FLAG, j].astype(jnp.float32)
            b_dense[group, j, half] = split(block)
            return carry

        lax.fori_loop(0, BAND, place, 0)

    def b_twin(u):
        send_b(4 + u, b_units[u], b_meta.at[u], twin)

    a_arrive(0)
    send_a(1, a_units.at[0], a_meta.at[0], zdev(turn))
    send_a(2, a_units.at[0], a_meta.at[0], zdev(-turn))

    b_arrive(0)
    send_b(1, b_units[0], b_meta.at[0], ydev(turn))
    send_b(2, b_units[0], b_meta.at[0], ydev(-turn))
    b_twin(0)
    b_unpack(0)
    b_arrive(4)
    b_unpack(4)
    b_arrive(1)
    send_b(3, b_units[1], b_meta.at[1], ydev(turn))
    b_twin(1)
    b_arrive(2)
    b_twin(2)
    b_unpack(1)
    b_unpack(2)
    b_arrive(5)
    b_unpack(5)
    b_arrive(6)
    b_unpack(6)
    a_arrive(1)
    a_forward(1)
    a_arrive(2)
    a_forward(2)
    b_arrive(3)
    b_twin(3)
    b_unpack(3)
    b_arrive(7)
    b_unpack(7)

    def unit_row(t, way, core):
        step = jnp.where(t % 2 == 1, -((t + 1) // 2), t // 2)
        return 2 * ((z + way * step + 8) % 8) + core

    def merge(t):
        i = unit_row(t, turn, q)
        for h, j, step, box, sem in ((0, 1, 1, from_left, left_recv), (1, 2, -1, from_right, right_recv)):
            got(opposite.at[t, h], opp_send.at[t, h], opp_recv.at[t, h])
            merged[t, h] = opposite[t, h] + partial[t, j, h]
            remote(merged.at[t, h], box.at[i], mg_send.at[t, h], sem.at[i], xdev(step, h)).start()

    def finish(t):
        for core, way in ((q, turn), (1 - q, -turn)):
            i = unit_row(t, way, core)
            got(from_left.at[i], mg_send.at[0, 0], left_recv.at[i])
            got(from_right.at[i], mg_send.at[0, 0], right_recv.at[i])
            if core is q:
                own = partial[t, 3, q]
            else:
                got(from_twin.at[t], twin_send.at[t], twin_recv.at[t])
                own = from_twin[t]
            total = own + from_left[i] + from_right[i]
            out[pl.ds(pl.multiple_of(i * BS, BS), BS), :] = total.T

    def unit(t, carry):
        @pl.when(t >= 3)
        def _():
            a_arrive(t)

        @pl.when((t >= 3) & (t <= 5))
        def _():
            a_forward(t)

        for s in range(PER):
            part = split(a_units[t, s])
            weights[2 * s * BS : (2 * s + 1) * BS, :] = part
            weights[(2 * s + 1) * BS : (2 * s + 2) * BS, :] = part
        places = [a_idx[t, LIST, s] for s in range(PER)]
        i = unit_row(t, turn, q)
        for j, step in enumerate((2, 1, 3, 0)):
            group = (x + step) % 4
            left = jnp.concatenate(
                [b_dense[group, place].reshape(2 * BS, 2 * BS) for place in places], axis=1
            )
            both = jnp.dot(left, weights[...], preferred_element_type=jnp.float32)
            both = both[:, :BS] + both[:, BS:]
            partial[t, j, 0] = both[:BS]
            partial[t, j, 1] = both[BS:]
            if j == 0:
                for h, way in ((0, 1), (1, -1)):
                    remote(
                        partial.at[t, j, h], opposite.at[t, h], opp_send.at[t, h], opp_recv.at[t, h], xdev(way, q)
                    ).start()
            elif j == 1:
                remote(
                    partial.at[t, j, 1], from_left.at[i], un_send.at[t, 0], left_recv.at[i], xdev(1, 1)
                ).start()
            elif j == 2:
                remote(
                    partial.at[t, j, 0], from_right.at[i], un_send.at[t, 1], right_recv.at[i], xdev(-1, 0)
                ).start()
            else:
                remote(
                    partial.at[t, j, 1 - q], from_twin.at[t], twin_send.at[t], twin_recv.at[t], twin
                ).start()

        @pl.when(t >= 1)
        def _():
            merge(t - 1)

        @pl.when(t >= 3)
        def _():
            finish(t - 3)

        return carry

    lax.fori_loop(0, UNITS, unit, 0)
    merge(UNITS - 1)

    def last(t, carry):
        finish(t)
        return carry

    lax.fori_loop(UNITS - 3, UNITS, last, 0)

    @pl.when(jnp.logical_not(a_self))
    def _():
        sent(a_meta.at[0], am_send.at[0], am_recv.at[0])
        sent(a_units.at[0], a_send.at[0], a_recv.at[0])

    @pl.when(jnp.logical_not(b_self))
    def _():
        sent(b_meta.at[0], bm_send.at[0], bm_recv.at[0])
        sent(b_units[0], b_send.at[0], b_recv.at[0])

    for k in range(1, UNITS):
        sent(a_meta.at[k], am_send.at[k], am_recv.at[k])
        sent(a_units.at[k], a_send.at[k], a_recv.at[k])
        sent(b_meta.at[k], bm_send.at[k], bm_recv.at[k])
        sent(b_units[k], b_send.at[k], b_recv.at[k])

    def drain(t, carry):
        for h in range(2):
            sent(opposite.at[t, h], opp_send.at[t, h], opp_recv.at[t, h])
            sent(merged.at[t, h], mg_send.at[t, h], opp_recv.at[t, h])
            sent(merged.at[t, h], un_send.at[t, h], opp_recv.at[t, h])
        sent(from_twin.at[t], twin_send.at[t], twin_recv.at[t])
        return carry

    lax.fori_loop(0, UNITS, drain, 0)


def shards(matrix, pattern):
    f32, i32 = jnp.float32, jnp.int32
    meta = index_tile(pattern)
    dma = pltpu.SemaphoreType.DMA
    return pl.pallas_call(
        kernel,
        out_shape=jax.ShapeDtypeStruct(matrix.shape, f32),
        in_specs=[
            pl.BlockSpec(memory_space=pltpu.VMEM),
            pl.BlockSpec(memory_space=pltpu.SMEM),
            pl.BlockSpec(memory_space=pltpu.VMEM),
        ],
        out_specs=pl.BlockSpec(memory_space=pltpu.VMEM),
        scratch_shapes=[
            pltpu.VMEM((PER, BS, BS), f32),
            pltpu.VMEM((PER, BS, BS), f32),
            pltpu.VMEM((UNITS, PER, BS, BS), f32),
            pltpu.VMEM((UNITS, 8, 128), i32),
            pltpu.SMEM((UNITS, 8, 128), i32),
            pltpu.VMEM((UNITS, 8, 128), i32),
            pltpu.SMEM((UNITS, 8, 128), i32),
            pltpu.VMEM((4, BAND, 2, BS, 2 * BS), jnp.bfloat16),
            pltpu.VMEM((PER * 2 * BS, 2 * BS), jnp.bfloat16),
            pltpu.VMEM((UNITS, 4, 2, BS, BS), f32),
            pltpu.VMEM((UNITS, 2, BS, BS), f32),
            pltpu.VMEM((UNITS, 2, BS, BS), f32),
            pltpu.VMEM((BAND, BS, BS), f32),
            pltpu.VMEM((BAND, BS, BS), f32),
            pltpu.VMEM((UNITS, BS, BS), f32),
        ]
        + [dma((UNITS,))] * 8
        + [dma]
        + [dma((UNITS, 2))] * 4
        + [dma((BAND,))] * 2
        + [dma((UNITS,))] * 2
        + [pltpu.VMEM((PER, BS, BS), f32)] * UNITS,
        compiler_params=pltpu.CompilerParams(
            collective_id=0, has_side_effects=True, vmem_limit_bytes=52 * 1024 * 1024
        ),
    )(matrix.reshape(BAND, BS, BS), meta, meta)


def solution(mesh):
    return jax.shard_map(
        shards,
        mesh=mesh,
        in_specs=(P("row", ("layer", "col")), P("row", ("layer", "col"))),
        out_specs=P("row", ("col", "layer")),
        check_vma=False,
    )
```

```python
import functools

import jax
import jax.numpy as jnp
from jax import lax
from jax.experimental import pallas as pl
from jax.experimental.pallas import tpu as pltpu
from jax.sharding import PartitionSpec as P

BS = 128
PER = 7
BAND = 16
UNITS = 8
LIST, SLOT, FLAG = 0, 1, 2


def index_tile(pattern):
    flags = pattern[:, 0]
    place = lax.broadcasted_iota(jnp.int32, (BAND, BAND), 0)
    upto = lax.broadcasted_iota(jnp.int32, (BAND, BAND), 1)
    count = jnp.sum(jnp.where(place <= upto, flags[:, None], 0), axis=0)
    order = lax.broadcasted_iota(jnp.int32, (BAND, BAND), 1)
    listed = jnp.sum((count[:, None] <= order).astype(jnp.int32), axis=0)
    rows = jnp.stack([jnp.minimum(listed, BAND - 1), jnp.clip(count - 1, 0, PER - 1), flags])
    return jnp.pad(rows, ((0, 8 - 3), (0, 128 - BAND)))


def split(value):
    high = value.astype(jnp.bfloat16)
    low = (value - high.astype(jnp.float32)).astype(jnp.bfloat16)
    return jnp.concatenate([high, low], axis=1)


def kernel(
    mat, meta_s, meta_v, out,
    packed, a_units, a_meta, a_idx, b_meta, b_idx, b_dense, weights,
    partial, merged, opposite, from_left, from_right, from_twin, done, passing,
    a_send, a_recv, am_send, am_recv, b_send, b_recv, bm_send, bm_recv, idx_sem,
    opp_send, opp_recv, mg_send, un_send, left_recv, right_recv, twin_send, twin_recv,
    done_send, pass_send, pass_recv, out_recv,
    *b_units,
):
    y, col, x = lax.axis_index("row"), lax.axis_index("col"), lax.axis_index("layer")
    z, q = col // 2, col % 2
    turn = 1 - 2 * q

    def at(row=None, col_=None, layer=None):
        return {
            "row": y if row is None else row,
            "col": col if col_ is None else col_,
            "layer": x if layer is None else layer,
        }

    def zdev(step):
        return at(col_=2 * ((z + step + 8) % 8) + q)

    def xdev(step):
        return at(layer=(x + step + 4) % 4)

    def ydev(step, core):
        return at(row=(y + step + 4) % 4, col_=2 * z + core)

    twin = at(col_=2 * z + 1 - q)

    barrier = pltpu.get_barrier_semaphore()

    def greet(device):
        pl.semaphore_signal(barrier, inc=1, device_id=device, device_id_type=pl.DeviceIdType.MESH)

    for device in (xdev(1), xdev(2), xdev(3), ydev(1, 0), ydev(1, 1), ydev(-1, 0), ydev(-1, 1)):
        greet(device)

    def greet_line(k, carry):
        greet(at(col_=(col + k) % BAND))
        return carry

    lax.fori_loop(1, BAND, greet_line, 0)

    for s in range(PER):
        block = mat[meta_s[LIST, s]]
        packed[s] = block
        b_units[0][s] = block.T
    own_idx = pltpu.make_async_copy(meta_v, a_idx.at[0], idx_sem)
    own_idx.start()
    own_idx.wait()

    pl.semaphore_wait(barrier, 7 + BAND - 1)

    def remote(src, dst, send, recv, device):
        return pltpu.make_async_remote_copy(
            src_ref=src, dst_ref=dst, send_sem=send, recv_sem=recv,
            device_id=device, device_id_type=pl.DeviceIdType.MESH,
        )

    def got(dst, send, recv):
        remote(dst, dst, send, recv, twin).wait_recv()

    def sent(src, send, recv):
        remote(src, src, send, recv, twin).wait_send()

    def send_a(t, data, meta, device):
        remote(meta, a_meta.at[t], am_send.at[t], am_recv.at[t], device).start()
        remote(data, a_units.at[t], a_send.at[t], a_recv.at[t], device).start()

    def send_b(u, data, meta, device):
        remote(meta, b_meta.at[u], bm_send.at[u], bm_recv.at[u], device).start()
        remote(data, b_units[u], b_send.at[u], b_recv.at[u], device).start()

    def a_arrive(t):
        got(a_meta.at[t], am_send.at[t], am_recv.at[t])
        index = pltpu.make_async_copy(a_meta.at[t], a_idx.at[t], idx_sem)
        index.start()
        got(a_units.at[t], a_send.at[t], a_recv.at[t])
        index.wait()

    def a_forward(t):
        way = jnp.where(t % 2 == 1, turn, -turn)
        send_a(t + 2, a_units.at[t], a_meta.at[t], zdev(way))

    def b_arrive(u):
        got(b_meta.at[u], bm_send.at[u], bm_recv.at[u])
        index = pltpu.make_async_copy(b_meta.at[u], b_idx.at[u], idx_sem)
        index.start()
        got(b_units[u], b_send.at[u], b_recv.at[u])
        index.wait()

    def b_unpack(u):
        way, core = (turn, q) if u < 4 else (-turn, 1 - q)
        group = (x + way * (0, -1, 1, -2)[u % 4] + 4) % 4

        def place(j, carry):
            slot = a_idx[0, SLOT, j] if u == 0 else b_idx[u, SLOT, j]
            flag = a_idx[0, FLAG, j] if u == 0 else b_idx[u, FLAG, j]
            b_dense[group, j, core] = split(b_units[u][slot] * flag.astype(jnp.float32))
            return carry

        lax.fori_loop(0, BAND, place, 0)

    def b_twin(u):
        send_b(4 + u, b_units[u], meta_v if u == 0 else b_meta.at[u], twin)

    send_b(1, b_units[0], meta_v, xdev(turn))
    send_b(2, b_units[0], meta_v, xdev(-turn))
    send_a(1, packed, meta_v, zdev(turn))
    send_a(2, packed, meta_v, zdev(-turn))
    b_twin(0)
    b_unpack(0)
    b_arrive(4)
    b_unpack(4)
    b_arrive(1)
    send_b(3, b_units[1], b_meta.at[1], xdev(turn))
    b_twin(1)
    b_arrive(2)
    b_twin(2)
    a_arrive(1)
    a_forward(1)
    a_arrive(2)
    a_forward(2)
    b_unpack(1)
    b_unpack(2)
    b_arrive(5)
    b_unpack(5)
    b_arrive(6)
    b_unpack(6)
    b_arrive(3)
    b_twin(3)
    b_unpack(3)
    b_arrive(7)
    b_unpack(7)

    def unit_row(t, way, core):
        step = jnp.where(t % 2 == 1, -((t + 1) // 2), t // 2)
        return 2 * ((z + way * step + 8) % 8) + core

    def merge(t):
        i = unit_row(t, turn, q)
        for h, j, step, box, sem in ((0, 1, 1, from_left, left_recv), (1, 2, -1, from_right, right_recv)):
            got(opposite.at[t, h], opp_send.at[t, h], opp_recv.at[t, h])
            merged[t, h] = opposite[t, h] + partial[t, j, h]
            remote(merged.at[t, h], box.at[i], mg_send.at[t, h], sem.at[i], ydev(step, h)).start()

    def block_out(k):
        return out.at[pl.ds(pl.multiple_of(k * BS, BS), BS), :]

    def deliver(value, src, m, step, send):
        owner = 4 * ((x + step) % 4) + m

        @pl.when(owner == col)
        def _():
            block_out(col)[...] = value[...]

        @pl.when(owner != col)
        def _():
            remote(src, block_out(col), send, out_recv.at[col], at(col_=owner)).start()

    def relay(t):
        for core, way in ((q, turn), (1 - q, -turn)):
            i = unit_row(t, way, core)
            m = i // 4

            @pl.when(i % 4 == x)
            def _():
                for step in (1, 3, 2):
                    box = passing.at[m, step - 1]
                    got(box, done_send.at[i], pass_recv.at[m, step - 1])
                    deliver(box, box, m, step, pass_send.at[m, step - 1])

    def finish(t):
        for core, way in ((q, turn), (1 - q, -turn)):
            i = unit_row(t, way, core)
            got(from_left.at[i], mg_send.at[0, 0], left_recv.at[i])
            got(from_right.at[i], mg_send.at[0, 0], right_recv.at[i])
            if core is q:
                own = partial[t, 3, q]
            else:
                got(from_twin.at[t], twin_send.at[t], twin_recv.at[t])
                own = from_twin[t]
            total = own + from_left[i] + from_right[i]
            done[i] = total
            m, step = i // 4, (x - i + 16) % 4

            @pl.when(step == 0)
            def _():
                deliver(done.at[i], done.at[i], m, 0, done_send.at[i])

            @pl.when(step != 0)
            def _():
                remote(
                    done.at[i], passing.at[m, step - 1], done_send.at[i], pass_recv.at[m, step - 1], at(layer=i % 4)
                ).start()

    def unit(t, carry):
        @pl.when(t >= 3)
        def _():
            a_arrive(t)

        @pl.when((t >= 3) & (t <= 5))
        def _():
            a_forward(t)

        def weigh(load):
            for s in range(PER):
                part = split(load(s))
                weights[2 * s * BS : (2 * s + 1) * BS, :] = part
                weights[(2 * s + 1) * BS : (2 * s + 2) * BS, :] = part

        @pl.when(t == 0)
        def _():
            weigh(lambda s: packed[s])

        @pl.when(t > 0)
        def _():
            weigh(lambda s: a_units[t, s])

        places = [a_idx[t, LIST, s] for s in range(PER)]
        i = unit_row(t, turn, q)
        for j, step in enumerate((2, 1, 3, 0)):
            group = (y + step) % 4
            left = jnp.concatenate(
                [b_dense[group, place].reshape(2 * BS, 2 * BS) for place in places], axis=1
            )
            both = jnp.dot(left, weights[...], preferred_element_type=jnp.float32)
            both = both[:, :BS] + both[:, BS:]
            partial[t, j, 0] = both[:BS]
            partial[t, j, 1] = both[BS:]
            if j == 0:
                for h, way in ((0, 1), (1, -1)):
                    remote(
                        partial.at[t, j, h], opposite.at[t, h], opp_send.at[t, h], opp_recv.at[t, h], ydev(way, q)
                    ).start()
            elif j == 1:
                remote(
                    partial.at[t, j, 1], from_left.at[i], un_send.at[t, 0], left_recv.at[i], ydev(1, 1)
                ).start()
            elif j == 2:
                remote(
                    partial.at[t, j, 0], from_right.at[i], un_send.at[t, 1], right_recv.at[i], ydev(-1, 0)
                ).start()
            else:
                remote(
                    partial.at[t, j, 1 - q], from_twin.at[t], twin_send.at[t], twin_recv.at[t], twin
                ).start()

        @pl.when(t >= 1)
        def _():
            merge(t - 1)

        @pl.when(t >= 3)
        def _():
            finish(t - 3)

        @pl.when(t >= 4)
        def _():
            relay(t - 4)

        return carry

    lax.fori_loop(0, UNITS, unit, 0)
    merge(UNITS - 1)

    def last(t, carry):
        finish(t)
        relay(t - 1)
        return carry

    lax.fori_loop(UNITS - 3, UNITS, last, 0)

    relay(UNITS - 1)

    for k in range(1, UNITS):
        sent(a_meta.at[k], am_send.at[k], am_recv.at[k])
        sent(a_units.at[k], a_send.at[k], a_recv.at[k])
        sent(b_meta.at[k], bm_send.at[k], bm_recv.at[k])
        sent(b_units[k], b_send.at[k], b_recv.at[k])

    def drain(t, carry):
        for h in range(2):
            sent(opposite.at[t, h], opp_send.at[t, h], opp_recv.at[t, h])
            sent(merged.at[t, h], mg_send.at[t, h], opp_recv.at[t, h])
            sent(merged.at[t, h], un_send.at[t, h], opp_recv.at[t, h])
        sent(from_twin.at[t], twin_send.at[t], twin_recv.at[t])
        return carry

    lax.fori_loop(0, UNITS, drain, 0)

    def collect(k, carry):
        @pl.when((k % 4 != x) | (4 * x + k // 4 != col))
        def _():
            sent(done.at[k], done_send.at[k], out_recv.at[k])

        @pl.when(k != col)
        def _():
            got(block_out(k), done_send.at[k], out_recv.at[k])

        for step in (1, 2, 3):
            @pl.when((k < 4) & (4 * ((x + step) % 4) + k != col))
            def _():
                m = lax.rem(k, 4)
                sent(passing.at[m, step - 1], pass_send.at[m, step - 1], out_recv.at[k])

        return carry

    lax.fori_loop(0, BAND, collect, 0)


def shards(matrix, pattern):
    f32, i32 = jnp.float32, jnp.int32
    meta = index_tile(pattern)
    dma = pltpu.SemaphoreType.DMA
    return pl.pallas_call(
        kernel,
        out_shape=jax.ShapeDtypeStruct(matrix.shape, f32),
        in_specs=[
            pl.BlockSpec(memory_space=pltpu.VMEM),
            pl.BlockSpec(memory_space=pltpu.SMEM),
            pl.BlockSpec(memory_space=pltpu.VMEM),
        ],
        out_specs=pl.BlockSpec(memory_space=pltpu.VMEM),
        scratch_shapes=[
            pltpu.VMEM((PER, BS, BS), f32),
            pltpu.VMEM((UNITS, PER, BS, BS), f32),
            pltpu.VMEM((UNITS, 8, 128), i32),
            pltpu.SMEM((UNITS, 8, 128), i32),
            pltpu.VMEM((UNITS, 8, 128), i32),
            pltpu.SMEM((UNITS, 8, 128), i32),
            pltpu.VMEM((4, BAND, 2, BS, 2 * BS), jnp.bfloat16),
            pltpu.VMEM((PER * 2 * BS, 2 * BS), jnp.bfloat16),
            pltpu.VMEM((UNITS, 4, 2, BS, BS), f32),
            pltpu.VMEM((UNITS, 2, BS, BS), f32),
            pltpu.VMEM((UNITS, 2, BS, BS), f32),
            pltpu.VMEM((BAND, BS, BS), f32),
            pltpu.VMEM((BAND, BS, BS), f32),
            pltpu.VMEM((UNITS, BS, BS), f32),
            pltpu.VMEM((BAND, BS, BS), f32),
            pltpu.VMEM((4, 3, BS, BS), f32),
        ]
        + [dma((UNITS,))] * 8
        + [dma]
        + [dma((UNITS, 2))] * 4
        + [dma((BAND,))] * 2
        + [dma((UNITS,))] * 2
        + [dma((BAND,)), dma((4, 3)), dma((4, 3)), dma((BAND,))]
        + [pltpu.VMEM((PER, BS, BS), f32)] * UNITS,
        compiler_params=pltpu.CompilerParams(
            collective_id=0, has_side_effects=True, vmem_limit_bytes=52 * 1024 * 1024
        ),
    )(matrix.reshape(BAND, BS, BS), meta, meta)


def solution(mesh):
    return jax.shard_map(
        shards,
        mesh=mesh,
        in_specs=(P("row", ("layer", "col")), P("row", ("layer", "col"))),
        out_specs=P("row", ("col", "layer")),
        check_vma=False,
    )
```

```python
import functools

import jax
import jax.numpy as jnp
from jax import lax
from jax.experimental import pallas as pl
from jax.experimental.pallas import tpu as pltpu
from jax.sharding import PartitionSpec as P

BS = 128
PER = 7
BAND = 16
UNITS = 8
PARTS = ((0, 4), (4, 3))
LIST, SLOT, FLAG = 0, 1, 2


def index_tile(pattern):
    flags = pattern[:, 0]
    place = lax.broadcasted_iota(jnp.int32, (BAND, BAND), 0)
    upto = lax.broadcasted_iota(jnp.int32, (BAND, BAND), 1)
    count = jnp.sum(jnp.where(place <= upto, flags[:, None], 0), axis=0)
    order = lax.broadcasted_iota(jnp.int32, (BAND, BAND), 1)
    listed = jnp.sum((count[:, None] <= order).astype(jnp.int32), axis=0)
    rows = jnp.stack([jnp.minimum(listed, BAND - 1), jnp.clip(count - 1, 0, PER - 1), flags])
    return jnp.pad(rows, ((0, 8 - 3), (0, 128 - BAND)))


def split(value):
    high = value.astype(jnp.bfloat16)
    low = (value - high.astype(jnp.float32)).astype(jnp.bfloat16)
    return jnp.concatenate([high, low], axis=1)


def kernel(
    mat, meta_s, meta_v, out,
    packed, a_units, a_meta, a_idx, b_meta, b_idx, b_dense, weights,
    partial, merged, opposite, from_left, from_right, from_twin, done, passing,
    a_send, a_recv, am_send, am_recv, b_send, b_recv, bm_send, bm_recv, idx_sem, b_idx_sem,
    opp_send, opp_recv, mg_send, un_send, left_recv, right_recv, twin_send, twin_recv,
    done_send, pass_send, pass_recv, out_recv,
    *b_units,
):
    y, col, x = lax.axis_index("row"), lax.axis_index("col"), lax.axis_index("layer")
    z, q = col // 2, col % 2
    turn = 1 - 2 * q

    def at(row=None, col_=None, layer=None):
        return {
            "row": y if row is None else row,
            "col": col if col_ is None else col_,
            "layer": x if layer is None else layer,
        }

    def zdev(step):
        return at(col_=2 * ((z + step + 8) % 8) + q)

    def xdev(step):
        return at(layer=(x + step + 4) % 4)

    def ydev(step, core):
        return at(row=(y + step + 4) % 4, col_=2 * z + core)

    twin = at(col_=2 * z + 1 - q)

    barrier = pltpu.get_barrier_semaphore()

    def greet(device):
        pl.semaphore_signal(barrier, inc=1, device_id=device, device_id_type=pl.DeviceIdType.MESH)

    for device in (ydev(1, 0), ydev(1, 1), ydev(-1, 0), ydev(-1, 1)):
        greet(device)
    for step in (1, 2, 3):
        greet(xdev(step))
        greet(at(col_=2 * z + 1 - q, layer=(x + step) % 4))

    def greet_line(k, carry):
        greet(at(col_=(col + k) % BAND))
        return carry

    lax.fori_loop(1, BAND, greet_line, 0)

    for s in range(PER):
        block = mat[meta_s[LIST, s]]
        packed[s] = block
        b_units[0][s] = block.T
    own_idx = pltpu.make_async_copy(meta_v, a_idx.at[0], idx_sem)
    own_idx.start()
    own_idx.wait()

    pl.semaphore_wait(barrier, 10 + BAND - 1)

    def remote(src, dst, send, recv, device):
        return pltpu.make_async_remote_copy(
            src_ref=src, dst_ref=dst, send_sem=send, recv_sem=recv,
            device_id=device, device_id_type=pl.DeviceIdType.MESH,
        )

    def got(dst, send, recv):
        remote(dst, dst, send, recv, twin).wait_recv()

    def sent(src, send, recv):
        remote(src, src, send, recv, twin).wait_send()

    def part_of(unit, part):
        return unit.at[pl.ds(*PARTS[part])]

    def send_a(t, part, data, device):
        remote(
            part_of(data, part), part_of(a_units.at[t], part), a_send.at[t, part], a_recv.at[t, part], device
        ).start()

    def send_b(u, data, device):
        remote(data, b_units[u], b_send.at[u], b_recv.at[u], device).start()

    def a_arrive(t, part):
        got(part_of(a_units.at[t], part), a_send.at[t, part], a_recv.at[t, part])

    def a_forward(t, part):
        way = jnp.where(t % 2 == 1, turn, -turn)
        send_a(t + 2, part, a_units.at[t], zdev(way))

    def b_arrive(u):
        got(b_units[u], b_send.at[u], b_recv.at[u])

    for t in range(1, UNITS):
        step = -((t + 1) // 2) if t % 2 else t // 2
        remote(meta_v, a_meta.at[t], am_send.at[t], am_recv.at[t], zdev(-turn * step)).start()
    for u in range(1, UNITS):
        step = (0, -1, 1, -2)[u % 4]
        device = at(col_=2 * z + (q if u < 4 else 1 - q), layer=(x - turn * step + 8) % 4)
        remote(meta_v, b_meta.at[u], bm_send.at[u], bm_recv.at[u], device).start()

    def indices():
        for k in range(1, UNITS):
            got(a_meta.at[k], am_send.at[k], am_recv.at[k])
            got(b_meta.at[k], bm_send.at[k], bm_recv.at[k])
        copies = [
            pltpu.make_async_copy(a_meta.at[pl.ds(1, UNITS - 1)], a_idx.at[pl.ds(1, UNITS - 1)], idx_sem),
            pltpu.make_async_copy(b_meta.at[pl.ds(1, UNITS - 1)], b_idx.at[pl.ds(1, UNITS - 1)], b_idx_sem),
        ]
        for copy in copies:
            copy.start()
        for copy in copies:
            copy.wait()

    def b_unpack(u):
        way, core = (turn, q) if u < 4 else (-turn, 1 - q)
        group = (x + way * (0, -1, 1, -2)[u % 4] + 4) % 4

        def place(j, carry):
            slot = a_idx[0, SLOT, j] if u == 0 else b_idx[u, SLOT, j]
            flag = a_idx[0, FLAG, j] if u == 0 else b_idx[u, FLAG, j]
            b_dense[group, j, core] = split(b_units[u][slot] * flag.astype(jnp.float32))
            return carry

        lax.fori_loop(0, BAND, place, 0)

    def b_twin(u):
        send_b(4 + u, b_units[u], twin)

    def unit_row(t, way, core):
        step = jnp.where(t % 2 == 1, -((t + 1) // 2), t // 2)
        return 2 * ((z + way * step + 8) % 8) + core

    def roles(off):
        group = (x + off) % 4
        return group, (group - y + 4) % 4

    def weigh(t, load):
        for s in range(PER):
            part = split(load(s))
            weights[t, 2 * s * BS : (2 * s + 1) * BS, :] = part
            weights[t, (2 * s + 1) * BS : (2 * s + 2) * BS, :] = part

    def chunk(t, off):
        group, role = roles(off)
        i = unit_row(t, turn, q)
        places = [a_idx[t, LIST, s] for s in range(PER)]
        left = jnp.concatenate([b_dense[group, place].reshape(2 * BS, 2 * BS) for place in places], axis=1)
        both = jnp.dot(left, weights[t], preferred_element_type=jnp.float32)
        both = both[:, :BS] + both[:, BS:]
        partial[t, role, 0] = both[:BS]
        partial[t, role, 1] = both[BS:]

        @pl.when(role == 2)
        def _():
            for h, way in ((0, 1), (1, -1)):
                remote(
                    partial.at[t, 2, h], opposite.at[t, h], opp_send.at[t, h], opp_recv.at[t, h], ydev(way, q)
                ).start()

        @pl.when(role == 1)
        def _():
            remote(partial.at[t, 1, 1], from_left.at[i], un_send.at[t, 0], left_recv.at[i], ydev(1, 1)).start()

        @pl.when(role == 3)
        def _():
            remote(partial.at[t, 3, 0], from_right.at[i], un_send.at[t, 1], right_recv.at[i], ydev(-1, 0)).start()

        @pl.when(role == 0)
        def _():
            remote(partial.at[t, 0, 1 - q], from_twin.at[t], twin_send.at[t], twin_recv.at[t], twin).start()

    def merge(t, off):
        i = unit_row(t, turn, q)
        for h, mine, step, box, sem in ((0, 1, 1, from_left, left_recv), (1, 3, -1, from_right, right_recv)):
            @pl.when(roles(off)[1] == mine)
            def _():
                got(opposite.at[t, h], opp_send.at[t, h], opp_recv.at[t, h])
                merged[t, h] = opposite[t, h] + partial[t, mine, h]
                remote(merged.at[t, h], box.at[i], mg_send.at[t, h], sem.at[i], ydev(step, h)).start()

    def block_out(k):
        return out.at[pl.ds(pl.multiple_of(k * BS, BS), BS), :]

    def deliver(value, src, m, step, send):
        owner = 4 * ((x + step) % 4) + m

        @pl.when(owner == col)
        def _():
            block_out(col)[...] = value[...]

        @pl.when(owner != col)
        def _():
            remote(src, block_out(col), send, out_recv.at[col], at(col_=owner)).start()

    def relay(t, late):
        for core, way in ((q, turn), (1 - q, -turn)):
            i = unit_row(t, way, core)
            m = i // 4

            @pl.when((i % 4 == x) & (((x - y + 4) % 4 == 2) == late))
            def _():
                deliver(done.at[i], done.at[i], m, 0, done_send.at[i])

            for step in (1, 3, 2):
                @pl.when((i % 4 == x) & (((x + step - y + 4) % 4 == 2) == late))
                def _():
                    box = passing.at[m, step - 1]
                    got(box, done_send.at[i], pass_recv.at[m, step - 1])
                    deliver(box, box, m, step, pass_send.at[m, step - 1])

    def finish(t, late):
        @pl.when(((y - x + 4) % 4 == 2) == late)
        def _():
            finish_now(t)

    def finish_now(t):
        for core, way in ((q, turn), (1 - q, -turn)):
            i = unit_row(t, way, core)
            got(from_left.at[i], mg_send.at[0, 0], left_recv.at[i])
            got(from_right.at[i], mg_send.at[0, 0], right_recv.at[i])
            if core is q:
                own = partial[t, 0, q]
            else:
                got(from_twin.at[t], twin_send.at[t], twin_recv.at[t])
                own = from_twin[t]
            total = own + from_left[i] + from_right[i]
            done[i] = total
            m, step = i // 4, (x - i + 16) % 4

            @pl.when(step != 0)
            def _():
                remote(
                    done.at[i], passing.at[m, step - 1], done_send.at[i], pass_recv.at[m, step - 1], at(layer=i % 4)
                ).start()

    def each(first, stop, *steps):
        def body(t, carry):
            for step in steps:
                step(t)
            return carry

        lax.fori_loop(first, stop, body, 0)

    def chunks(*offs):
        return [functools.partial(chunk, off=off) for off in offs]

    def merges(*offs):
        return [functools.partial(merge, off=off) for off in offs]

    def finishes(late):
        return [functools.partial(finish, late=late)]

    def relays(late):
        return [functools.partial(relay, late=late)]

    def weigh_unit(t):
        weigh(t, lambda s: a_units[t, s])

    def pass_on(first, stop, part):
        each(
            first, stop, functools.partial(a_arrive, part=part), functools.partial(a_forward, part=part)
        )

    for part in range(2):
        send_a(1, part, packed, zdev(turn))
        send_a(2, part, packed, zdev(-turn))
    send_b(1, b_units[0], xdev(turn))
    send_b(2, b_units[0], xdev(-turn))
    indices()
    weigh(0, lambda s: packed[s])
    pass_on(1, 3, 0)
    b_twin(0)
    b_unpack(0)
    b_arrive(4)
    b_arrive(1)
    b_twin(1)
    send_b(3, b_units[1], xdev(turn))
    pass_on(1, 3, 1)
    b_arrive(2)
    b_unpack(4)
    each(1, 3, weigh_unit)
    chunk(0, 0)
    b_twin(2)
    b_unpack(2)
    b_unpack(1)
    each(1, 3, *chunks(0))
    b_arrive(6)
    b_unpack(6)
    b_arrive(5)
    b_unpack(5)
    each(0, 3, *chunks(1, 3))
    pass_on(3, 5, 0)
    each(1, 3, *merges(0))
    pass_on(3, 5, 1)
    merge(0, 0)
    each(0, 3, *merges(1, 3))
    b_arrive(3)
    b_twin(3)
    b_unpack(3)
    each(3, 5, weigh_unit)
    b_arrive(7)
    b_unpack(7)
    each(3, 5, *chunks(2, 0, 1, 3))
    pass_on(5, 6, 0)
    a_arrive(6, 0)
    each(0, 3, *finishes(False))
    a_arrive(6, 1)
    pass_on(5, 6, 1)
    each(3, 5, *merges(2))
    each(5, 7, weigh_unit)
    each(5, 7, *chunks(2, 0, 1, 3))
    each(3, 5, *merges(0, 1, 3))
    each(3, 5, *finishes(True))
    each(0, 3, *relays(False))
    a_arrive(7, 0)
    each(5, 7, *merges(0, 1, 3))
    each(5, 7, *merges(2))
    a_arrive(7, 1)
    each(7, 8, weigh_unit, *chunks(2, 0, 1, 3))
    each(3, 5, *relays(True))
    each(3, 5, *finishes(False))
    each(0, 3, *chunks(2))
    each(5, 7, *finishes(False))
    each(5, 7, *finishes(True))
    each(7, 8, *merges(2))
    each(3, 5, *relays(False))
    each(5, 7, *relays(True))
    each(7, 8, *merges(0, 1, 3))
    each(0, 3, *merges(2))
    each(5, 7, *relays(False))
    each(7, 8, *finishes(False))
    each(7, 8, *finishes(True))
    each(7, 8, *relays(True))
    each(0, 3, *finishes(True))
    each(7, 8, *relays(False))
    each(0, 3, *relays(True))

    for k in range(1, UNITS):
        sent(a_meta.at[k], am_send.at[k], am_recv.at[k])
        for part in range(2):
            sent(part_of(a_units.at[k], part), a_send.at[k, part], a_recv.at[k, part])
        sent(b_meta.at[k], bm_send.at[k], bm_recv.at[k])
        sent(b_units[k], b_send.at[k], b_recv.at[k])

    def drain(t, carry):
        for h in range(2):
            sent(opposite.at[t, h], opp_send.at[t, h], opp_recv.at[t, h])
            sent(merged.at[t, h], mg_send.at[t, h], opp_recv.at[t, h])
            sent(merged.at[t, h], un_send.at[t, h], opp_recv.at[t, h])
        sent(from_twin.at[t], twin_send.at[t], twin_recv.at[t])
        return carry

    lax.fori_loop(0, UNITS, drain, 0)

    def collect(k, carry):
        @pl.when((k % 4 != x) | (4 * x + k // 4 != col))
        def _():
            sent(done.at[k], done_send.at[k], out_recv.at[k])

        @pl.when(k != col)
        def _():
            got(block_out(k), done_send.at[k], out_recv.at[k])

        for step in (1, 2, 3):
            @pl.when((k < 4) & (4 * ((x + step) % 4) + k != col))
            def _():
                m = lax.rem(k, 4)
                sent(passing.at[m, step - 1], pass_send.at[m, step - 1], out_recv.at[k])

        return carry

    lax.fori_loop(0, BAND, collect, 0)


def shards(matrix, pattern):
    f32, i32 = jnp.float32, jnp.int32
    meta = index_tile(pattern)
    dma = pltpu.SemaphoreType.DMA
    return pl.pallas_call(
        kernel,
        out_shape=jax.ShapeDtypeStruct(matrix.shape, f32),
        in_specs=[
            pl.BlockSpec(memory_space=pltpu.VMEM),
            pl.BlockSpec(memory_space=pltpu.SMEM),
            pl.BlockSpec(memory_space=pltpu.VMEM),
        ],
        out_specs=pl.BlockSpec(memory_space=pltpu.VMEM),
        scratch_shapes=[
            pltpu.VMEM((PER, BS, BS), f32),
            pltpu.VMEM((UNITS, PER, BS, BS), f32),
            pltpu.VMEM((UNITS, 8, 128), i32),
            pltpu.SMEM((UNITS, 8, 128), i32),
            pltpu.VMEM((UNITS, 8, 128), i32),
            pltpu.SMEM((UNITS, 8, 128), i32),
            pltpu.VMEM((4, BAND, 2, BS, 2 * BS), jnp.bfloat16),
            pltpu.VMEM((UNITS, PER * 2 * BS, 2 * BS), jnp.bfloat16),
            pltpu.VMEM((UNITS, 4, 2, BS, BS), f32),
            pltpu.VMEM((UNITS, 2, BS, BS), f32),
            pltpu.VMEM((UNITS, 2, BS, BS), f32),
            pltpu.VMEM((BAND, BS, BS), f32),
            pltpu.VMEM((BAND, BS, BS), f32),
            pltpu.VMEM((UNITS, BS, BS), f32),
            pltpu.VMEM((BAND, BS, BS), f32),
            pltpu.VMEM((4, 3, BS, BS), f32),
        ]
        + [dma((UNITS, 2))] * 2
        + [dma((UNITS,))] * 6
        + [dma] * 2
        + [dma((UNITS, 2))] * 4
        + [dma((BAND,))] * 2
        + [dma((UNITS,))] * 2
        + [dma((BAND,)), dma((4, 3)), dma((4, 3)), dma((BAND,))]
        + [pltpu.VMEM((PER, BS, BS), f32)] * UNITS,
        compiler_params=pltpu.CompilerParams(
            collective_id=0, has_side_effects=True, vmem_limit_bytes=52 * 1024 * 1024
        ),
    )(matrix.reshape(BAND, BS, BS), meta, meta)


def solution(mesh):
    return jax.shard_map(
        shards,
        mesh=mesh,
        in_specs=(P("row", ("layer", "col")), P("row", ("layer", "col"))),
        out_specs=P("row", ("col", "layer")),
        check_vma=False,
    )
```

```python
import functools

import jax
import jax.numpy as jnp
from jax import lax
from jax.experimental import pallas as pl
from jax.experimental.pallas import tpu as pltpu
from jax.sharding import PartitionSpec as P

BS = 128
PER = 7
BAND = 16
UNITS = 8
PARTS = ((0, 4), (4, 3))
LIST, SLOT, FLAG = 0, 1, 2


def index_lists(flags):
    counts, count = [], 0
    for flag in flags:
        count = count + flag
        counts.append(count)
    listed = [jnp.minimum(sum((c <= s).astype(jnp.int32) for c in counts), BAND - 1) for s in range(PER)]
    return listed, [jnp.clip(c - 1, 0, PER - 1) for c in counts]


def split(value):
    high = value.astype(jnp.bfloat16)
    low = (value - high.astype(jnp.float32)).astype(jnp.bfloat16)
    return jnp.concatenate([high, low], axis=1)


def kernel(
    pattern, matrix, out,
    mat, own, meta_v, packed, a_units, a_meta, a_idx, b_meta, b_idx, b_dense, weights,
    partial, merged, opposite, from_left, from_right, from_twin, done, passing,
    a_send, a_recv, am_send, am_recv, b_send, b_recv, bm_send, bm_recv, idx_sem, b_idx_sem,
    opp_send, opp_recv, mg_send, un_send, left_recv, right_recv, twin_send, twin_recv,
    done_send, pass_send, pass_recv, out_recv, mat_sem,
    *b_units,
):
    load = pltpu.make_async_copy(matrix, mat, mat_sem)
    load.start()
    flag_load = pltpu.make_async_copy(pattern, own, idx_sem)
    flag_load.start()
    y, col, x = lax.axis_index("row"), lax.axis_index("col"), lax.axis_index("layer")
    z, q = col // 2, col % 2
    turn = 1 - 2 * q

    def at(row=None, col_=None, layer=None):
        return {
            "row": y if row is None else row,
            "col": col if col_ is None else col_,
            "layer": x if layer is None else layer,
        }

    def zdev(step):
        return at(col_=2 * ((z + step + 8) % 8) + q)

    def xdev(step):
        return at(layer=(x + step + 4) % 4)

    def ydev(step, core):
        return at(row=(y + step + 4) % 4, col_=2 * z + core)

    twin = at(col_=2 * z + 1 - q)

    barrier = pltpu.get_barrier_semaphore()

    def greet(device):
        pl.semaphore_signal(barrier, inc=1, device_id=device, device_id_type=pl.DeviceIdType.MESH)

    for device in (ydev(1, 0), ydev(1, 1), ydev(-1, 0), ydev(-1, 1)):
        greet(device)
    for step in (1, 2, 3):
        greet(xdev(step))
        greet(at(col_=2 * z + 1 - q, layer=(x + step) % 4))

    def greet_line(k, carry):
        greet(at(col_=(col + k) % BAND))
        return carry

    lax.fori_loop(1, BAND, greet_line, 0)

    flag_load.wait()
    flags = [own[0, j] for j in range(BAND)]
    listed, slots = index_lists(flags)
    row, lane = (lax.broadcasted_iota(jnp.int32, (8, 128), d) for d in (0, 1))
    tile = jnp.zeros((8, 128), jnp.int32)
    for kind, values in ((LIST, listed), (SLOT, slots), (FLAG, flags)):
        for k, value in enumerate(values):
            tile = jnp.where((row == kind) & (lane == k), value, tile)
    meta_v[...] = tile
    load.wait()
    for s in range(PER):
        block = mat[listed[s]]
        packed[s] = block
        b_units[0][s] = block.T
    own_idx = pltpu.make_async_copy(meta_v, a_idx.at[0], idx_sem)
    own_idx.start()
    own_idx.wait()

    pl.semaphore_wait(barrier, 10 + BAND - 1)

    def remote(src, dst, send, recv, device):
        return pltpu.make_async_remote_copy(
            src_ref=src, dst_ref=dst, send_sem=send, recv_sem=recv,
            device_id=device, device_id_type=pl.DeviceIdType.MESH,
        )

    def got(dst, send, recv):
        remote(dst, dst, send, recv, twin).wait_recv()

    def sent(src, send, recv):
        remote(src, src, send, recv, twin).wait_send()

    def part_of(unit, part):
        return unit.at[pl.ds(*PARTS[part])]

    def send_a(t, part, data, device):
        remote(
            part_of(data, part), part_of(a_units.at[t], part), a_send.at[t, part], a_recv.at[t, part], device
        ).start()

    def send_b(u, data, device):
        remote(data, b_units[u], b_send.at[u], b_recv.at[u], device).start()

    def a_arrive(t, part):
        got(part_of(a_units.at[t], part), a_send.at[t, part], a_recv.at[t, part])

    def a_forward(t, part):
        way = jnp.where(t % 2 == 1, turn, -turn)
        send_a(t + 2, part, a_units.at[t], zdev(way))

    def b_arrive(u):
        got(b_units[u], b_send.at[u], b_recv.at[u])

    for t in range(1, UNITS):
        step = -((t + 1) // 2) if t % 2 else t // 2
        remote(meta_v, a_meta.at[t], am_send.at[t], am_recv.at[t], zdev(-turn * step)).start()
    for u in range(1, UNITS):
        step = (0, -1, 1, -2)[u % 4]
        device = at(col_=2 * z + (q if u < 4 else 1 - q), layer=(x - turn * step + 8) % 4)
        remote(meta_v, b_meta.at[u], bm_send.at[u], bm_recv.at[u], device).start()

    def indices():
        for k in range(1, UNITS):
            got(a_meta.at[k], am_send.at[k], am_recv.at[k])
            got(b_meta.at[k], bm_send.at[k], bm_recv.at[k])
        copies = [
            pltpu.make_async_copy(a_meta.at[pl.ds(1, UNITS - 1)], a_idx.at[pl.ds(1, UNITS - 1)], idx_sem),
            pltpu.make_async_copy(b_meta.at[pl.ds(1, UNITS - 1)], b_idx.at[pl.ds(1, UNITS - 1)], b_idx_sem),
        ]
        for copy in copies:
            copy.start()
        for copy in copies:
            copy.wait()

    def b_unpack(u):
        way, core = (turn, q) if u < 4 else (-turn, 1 - q)
        group = (x + way * (0, -1, 1, -2)[u % 4] + 4) % 4

        def place(j, carry):
            slot = a_idx[0, SLOT, j] if u == 0 else b_idx[u, SLOT, j]
            flag = a_idx[0, FLAG, j] if u == 0 else b_idx[u, FLAG, j]
            b_dense[group, j, core] = split(b_units[u][slot] * flag.astype(jnp.float32))
            return carry

        lax.fori_loop(0, BAND, place, 0)

    def b_twin(u):
        send_b(4 + u, b_units[u], twin)

    def unit_row(t, way, core):
        step = jnp.where(t % 2 == 1, -((t + 1) // 2), t // 2)
        return 2 * ((z + way * step + 8) % 8) + core

    def roles(off):
        group = (x + off) % 4
        return group, (group - y + 4) % 4

    def weigh(t, load):
        for s in range(PER):
            part = split(load(s))
            weights[t, 2 * s * BS : (2 * s + 1) * BS, :] = part
            weights[t, (2 * s + 1) * BS : (2 * s + 2) * BS, :] = part

    def chunk(t, off):
        group, role = roles(off)
        i = unit_row(t, turn, q)
        places = [a_idx[t, LIST, s] for s in range(PER)]
        left = jnp.concatenate([b_dense[group, place].reshape(2 * BS, 2 * BS) for place in places], axis=1)
        both = jnp.dot(left, weights[t], preferred_element_type=jnp.float32)
        both = both[:, :BS] + both[:, BS:]
        partial[t, role, 0] = both[:BS]
        partial[t, role, 1] = both[BS:]

        @pl.when(role == 2)
        def _():
            for h, way in ((0, 1), (1, -1)):
                remote(
                    partial.at[t, 2, h], opposite.at[t, h], opp_send.at[t, h], opp_recv.at[t, h], ydev(way, q)
                ).start()

        @pl.when(role == 1)
        def _():
            remote(partial.at[t, 1, 1], from_left.at[i], un_send.at[t, 0], left_recv.at[i], ydev(1, 1)).start()

        @pl.when(role == 3)
        def _():
            remote(partial.at[t, 3, 0], from_right.at[i], un_send.at[t, 1], right_recv.at[i], ydev(-1, 0)).start()

        @pl.when(role == 0)
        def _():
            remote(partial.at[t, 0, 1 - q], from_twin.at[t], twin_send.at[t], twin_recv.at[t], twin).start()

    def merge(t, off):
        i = unit_row(t, turn, q)
        for h, mine, step, box, sem in ((0, 1, 1, from_left, left_recv), (1, 3, -1, from_right, right_recv)):
            @pl.when(roles(off)[1] == mine)
            def _():
                got(opposite.at[t, h], opp_send.at[t, h], opp_recv.at[t, h])
                merged[t, h] = opposite[t, h] + partial[t, mine, h]
                remote(merged.at[t, h], box.at[i], mg_send.at[t, h], sem.at[i], ydev(step, h)).start()

    def block_out(k):
        return out.at[pl.ds(pl.multiple_of(k * BS, BS), BS), :]

    def deliver(value, src, m, step, send):
        owner = 4 * ((x + step) % 4) + m

        @pl.when(owner == col)
        def _():
            block_out(col)[...] = value[...]

        @pl.when(owner != col)
        def _():
            remote(src, block_out(col), send, out_recv.at[col], at(col_=owner)).start()

    def relay(t, late):
        for core, way in ((q, turn), (1 - q, -turn)):
            i = unit_row(t, way, core)
            m = i // 4

            @pl.when((i % 4 == x) & (((x - y + 4) % 4 == 2) == late))
            def _():
                deliver(done.at[i], done.at[i], m, 0, done_send.at[i])

            for step in (1, 3, 2):
                @pl.when((i % 4 == x) & (((x + step - y + 4) % 4 == 2) == late))
                def _():
                    box = passing.at[m, step - 1]
                    got(box, done_send.at[i], pass_recv.at[m, step - 1])
                    deliver(box, box, m, step, pass_send.at[m, step - 1])

    def finish(t, late):
        @pl.when(((y - x + 4) % 4 == 2) == late)
        def _():
            finish_now(t)

    def finish_now(t):
        for core, way in ((q, turn), (1 - q, -turn)):
            i = unit_row(t, way, core)
            got(from_left.at[i], mg_send.at[0, 0], left_recv.at[i])
            got(from_right.at[i], mg_send.at[0, 0], right_recv.at[i])
            if core is q:
                own = partial[t, 0, q]
            else:
                got(from_twin.at[t], twin_send.at[t], twin_recv.at[t])
                own = from_twin[t]
            total = own + from_left[i] + from_right[i]
            done[i] = total
            m, step = i // 4, (x - i + 16) % 4

            @pl.when(step != 0)
            def _():
                remote(
                    done.at[i], passing.at[m, step - 1], done_send.at[i], pass_recv.at[m, step - 1], at(layer=i % 4)
                ).start()

    def each(first, stop, *steps):
        def body(t, carry):
            for step in steps:
                step(t)
            return carry

        lax.fori_loop(first, stop, body, 0)

    def chunks(*offs):
        return [functools.partial(chunk, off=off) for off in offs]

    def all_chunks(first, stop):
        def body(n, carry):
            chunk(n // 4, (n + 2) % 4)
            return carry

        lax.fori_loop(4 * first, 4 * stop, body, 0)

    def merges(*offs):
        return [functools.partial(merge, off=off) for off in offs]

    def finishes(late):
        return [functools.partial(finish, late=late)]

    def relays(late):
        return [functools.partial(relay, late=late)]

    def weigh_unit(t):
        weigh(t, lambda s: a_units[t, s])

    def pass_on(first, stop, part):
        each(
            first, stop, functools.partial(a_arrive, part=part), functools.partial(a_forward, part=part)
        )

    for part in range(2):
        send_a(1, part, packed, zdev(turn))
        send_a(2, part, packed, zdev(-turn))
    send_b(1, b_units[0], xdev(turn))
    send_b(2, b_units[0], xdev(-turn))
    indices()
    weigh(0, lambda s: packed[s])
    pass_on(1, 3, 0)
    b_twin(0)
    b_unpack(0)
    b_arrive(4)
    b_arrive(1)
    b_twin(1)
    send_b(3, b_units[1], xdev(turn))
    pass_on(1, 3, 1)
    b_arrive(2)
    b_unpack(4)
    each(1, 3, weigh_unit)
    chunk(0, 0)
    b_twin(2)
    b_unpack(2)
    b_unpack(1)
    each(1, 3, *chunks(0))
    b_arrive(6)
    b_unpack(6)
    b_arrive(5)
    b_unpack(5)
    each(0, 3, *chunks(1, 3))
    pass_on(3, 5, 0)
    each(1, 3, *merges(0))
    pass_on(3, 5, 1)
    merge(0, 0)
    each(0, 3, *merges(1, 3))
    b_arrive(3)
    b_twin(3)
    b_unpack(3)
    each(3, 5, weigh_unit)
    b_arrive(7)
    b_unpack(7)
    all_chunks(3, 5)
    pass_on(5, 6, 0)
    a_arrive(6, 0)
    each(0, 3, *finishes(False))
    a_arrive(6, 1)
    pass_on(5, 6, 1)
    each(3, 5, *merges(2))
    each(5, 7, weigh_unit)
    all_chunks(5, 7)
    each(3, 5, *merges(0, 1, 3))
    each(3, 5, *finishes(True))
    each(0, 3, *relays(False))
    a_arrive(7, 0)
    each(5, 7, *merges(0, 1, 3))
    each(5, 7, *merges(2))
    a_arrive(7, 1)
    each(7, 8, weigh_unit)
    all_chunks(7, 8)
    each(3, 5, *relays(True))
    each(3, 5, *finishes(False))
    each(0, 3, *chunks(2))
    each(5, 7, *finishes(False))
    each(5, 7, *finishes(True))
    each(7, 8, *merges(2))
    each(3, 5, *relays(False))
    each(5, 7, *relays(True))
    each(7, 8, *merges(0, 1, 3))
    each(0, 3, *merges(2))
    each(5, 7, *relays(False))
    each(7, 8, *finishes(False))
    each(7, 8, *finishes(True))
    each(7, 8, *relays(True))
    each(0, 3, *finishes(True))
    each(7, 8, *relays(False))
    each(0, 3, *relays(True))

    for k in range(1, UNITS):
        sent(a_meta.at[k], am_send.at[k], am_recv.at[k])
        for part in range(2):
            sent(part_of(a_units.at[k], part), a_send.at[k, part], a_recv.at[k, part])
        sent(b_meta.at[k], bm_send.at[k], bm_recv.at[k])
        sent(b_units[k], b_send.at[k], b_recv.at[k])

    def drain(t, carry):
        for h in range(2):
            sent(opposite.at[t, h], opp_send.at[t, h], opp_recv.at[t, h])
            sent(merged.at[t, h], mg_send.at[t, h], opp_recv.at[t, h])
            sent(merged.at[t, h], un_send.at[t, h], opp_recv.at[t, h])
        sent(from_twin.at[t], twin_send.at[t], twin_recv.at[t])
        return carry

    lax.fori_loop(0, UNITS, drain, 0)

    def collect(k, carry):
        @pl.when((k % 4 != x) | (4 * x + k // 4 != col))
        def _():
            sent(done.at[k], done_send.at[k], out_recv.at[k])

        @pl.when(k != col)
        def _():
            got(block_out(k), done_send.at[k], out_recv.at[k])

        for step in (1, 2, 3):
            @pl.when((k < 4) & (4 * ((x + step) % 4) + k != col))
            def _():
                m = lax.rem(k, 4)
                sent(passing.at[m, step - 1], pass_send.at[m, step - 1], out_recv.at[k])

        return carry

    lax.fori_loop(0, BAND, collect, 0)


def shards(matrix, pattern):
    f32, i32 = jnp.float32, jnp.int32
    dma = pltpu.SemaphoreType.DMA
    return pl.pallas_call(
        kernel,
        out_shape=jax.ShapeDtypeStruct(matrix.shape, f32),
        in_specs=[
            pl.BlockSpec(memory_space=pl.ANY),
            pl.BlockSpec(memory_space=pl.ANY),
        ],
        out_specs=pl.BlockSpec(memory_space=pltpu.VMEM),
        scratch_shapes=[
            pltpu.VMEM((BAND, BS, BS), f32),
            pltpu.SMEM((1, BAND), i32),
            pltpu.VMEM((8, 128), i32),
            pltpu.VMEM((PER, BS, BS), f32),
            pltpu.VMEM((UNITS, PER, BS, BS), f32),
            pltpu.VMEM((UNITS, 8, 128), i32),
            pltpu.SMEM((UNITS, 8, 128), i32),
            pltpu.VMEM((UNITS, 8, 128), i32),
            pltpu.SMEM((UNITS, 8, 128), i32),
            pltpu.VMEM((4, BAND, 2, BS, 2 * BS), jnp.bfloat16),
            pltpu.VMEM((UNITS, PER * 2 * BS, 2 * BS), jnp.bfloat16),
            pltpu.VMEM((UNITS, 4, 2, BS, BS), f32),
            pltpu.VMEM((UNITS, 2, BS, BS), f32),
            pltpu.VMEM((UNITS, 2, BS, BS), f32),
            pltpu.VMEM((BAND, BS, BS), f32),
            pltpu.VMEM((BAND, BS, BS), f32),
            pltpu.VMEM((UNITS, BS, BS), f32),
            pltpu.VMEM((BAND, BS, BS), f32),
            pltpu.VMEM((4, 3, BS, BS), f32),
        ]
        + [dma((UNITS, 2))] * 2
        + [dma((UNITS,))] * 6
        + [dma] * 2
        + [dma((UNITS, 2))] * 4
        + [dma((BAND,))] * 2
        + [dma((UNITS,))] * 2
        + [dma((BAND,)), dma((4, 3)), dma((4, 3)), dma((BAND,)), dma]
        + [pltpu.VMEM((PER, BS, BS), f32)] * UNITS,
        compiler_params=pltpu.CompilerParams(
            collective_id=0, has_side_effects=True, vmem_limit_bytes=52 * 1024 * 1024
        ),
    )(pattern.reshape(1, BAND), matrix.reshape(BAND, BS, BS))


def solution(mesh):
    return jax.shard_map(
        shards,
        mesh=mesh,
        in_specs=(P("row", ("layer", "col")), P("row", ("layer", "col"))),
        out_specs=P("row", ("col", "layer")),
        check_vma=False,
    )
```

```python
import functools

import jax
import jax.numpy as jnp
from jax import lax
from jax.experimental import pallas as pl
from jax.experimental.pallas import tpu as pltpu
from jax.sharding import PartitionSpec as P

BS = 128
PER = 7
BAND = 16
UNITS = 8
PARTS = ((0, 4), (4, 3))
LIST, SLOT, FLAG = 0, 1, 2


def index_lists(flags):
    counts, count = [], 0
    for flag in flags:
        count = count + flag
        counts.append(count)
    listed = [jnp.minimum(sum((c <= s).astype(jnp.int32) for c in counts), BAND - 1) for s in range(PER)]
    return listed, [jnp.clip(c - 1, 0, PER - 1) for c in counts]


def split(value):
    high = value.astype(jnp.bfloat16)
    low = (value - high.astype(jnp.float32)).astype(jnp.bfloat16)
    return jnp.concatenate([high, low], axis=1)


def kernel(
    pattern, matrix, out,
    mat, own, meta_v, packed, a_units, a_meta, a_idx, b_meta, b_idx, b_dense, weights,
    partial, merged, opposite, from_left, from_right, from_twin, done, passing,
    a_send, a_recv, am_send, am_recv, b_send, b_recv, bm_send, bm_recv, idx_sem, b_idx_sem,
    opp_send, opp_recv, mg_send, un_send, left_recv, right_recv, twin_send, twin_recv,
    done_send, pass_send, pass_recv, out_recv, mat_sem,
    *b_units,
):
    load = pltpu.make_async_copy(matrix, mat, mat_sem)
    load.start()
    flag_load = pltpu.make_async_copy(pattern, own, idx_sem)
    flag_load.start()
    y, col, x = lax.axis_index("row"), lax.axis_index("col"), lax.axis_index("layer")
    z, q = col // 2, col % 2
    turn = 1 - 2 * q

    def at(row=None, col_=None, layer=None):
        return {
            "row": y if row is None else row,
            "col": col if col_ is None else col_,
            "layer": x if layer is None else layer,
        }

    def zdev(step):
        return at(col_=2 * ((z + step + 8) % 8) + q)

    def xdev(step):
        return at(layer=(x + step + 4) % 4)

    def ydev(step, core):
        return at(row=(y + step + 4) % 4, col_=2 * z + core)

    twin = at(col_=2 * z + 1 - q)

    barrier = pltpu.get_barrier_semaphore()

    def greet(device):
        pl.semaphore_signal(barrier, inc=1, device_id=device, device_id_type=pl.DeviceIdType.MESH)

    for device in (ydev(1, 0), ydev(1, 1), ydev(-1, 0), ydev(-1, 1)):
        greet(device)
    for step in (1, 2, 3):
        greet(xdev(step))
        greet(at(col_=2 * z + 1 - q, layer=(x + step) % 4))

    def greet_line(k, carry):
        greet(at(col_=(col + k) % BAND))
        return carry

    lax.fori_loop(1, BAND, greet_line, 0)

    flag_load.wait()
    flags = [own[0, j] for j in range(BAND)]
    listed, slots = index_lists(flags)
    row, lane = (lax.broadcasted_iota(jnp.int32, (8, 128), d) for d in (0, 1))
    tile = jnp.zeros((8, 128), jnp.int32)
    for kind, values in ((LIST, listed), (SLOT, slots), (FLAG, flags)):
        for k, value in enumerate(values):
            tile = jnp.where((row == kind) & (lane == k), value, tile)
    meta_v[...] = tile
    load.wait()
    for s in range(PER):
        block = mat[listed[s]]
        packed[s] = block
        b_units[0][s] = block.T
    own_idx = pltpu.make_async_copy(meta_v, a_idx.at[0], idx_sem)
    own_idx.start()
    own_idx.wait()

    pl.semaphore_wait(barrier, 10 + BAND - 1)

    def remote(src, dst, send, recv, device):
        return pltpu.make_async_remote_copy(
            src_ref=src, dst_ref=dst, send_sem=send, recv_sem=recv,
            device_id=device, device_id_type=pl.DeviceIdType.MESH,
        )

    def got(dst, send, recv):
        remote(dst, dst, send, recv, twin).wait_recv()

    def sent(src, send, recv):
        remote(src, src, send, recv, twin).wait_send()

    def part_of(unit, part):
        return unit.at[pl.ds(*PARTS[part])]

    def send_a(t, part, data, device):
        remote(
            part_of(data, part), part_of(a_units.at[t], part), a_send.at[t, part], a_recv.at[t, part], device
        ).start()

    def send_b(u, data, device):
        remote(data, b_units[u], b_send.at[u], b_recv.at[u], device).start()

    def a_arrive(t, part):
        got(part_of(a_units.at[t], part), a_send.at[t, part], a_recv.at[t, part])

    def a_forward(t, part):
        way = jnp.where(t % 2 == 1, turn, -turn)
        send_a(t + 2, part, a_units.at[t], zdev(way))

    def b_arrive(u):
        got(b_units[u], b_send.at[u], b_recv.at[u])

    for t in range(1, UNITS):
        step = -((t + 1) // 2) if t % 2 else t // 2
        remote(meta_v, a_meta.at[t], am_send.at[t], am_recv.at[t], zdev(-turn * step)).start()
    for u in range(1, UNITS):
        step = (0, -1, 1, -2)[u % 4]
        device = at(col_=2 * z + (q if u < 4 else 1 - q), layer=(x - turn * step + 8) % 4)
        remote(meta_v, b_meta.at[u], bm_send.at[u], bm_recv.at[u], device).start()

    def indices():
        for k in range(1, UNITS):
            got(a_meta.at[k], am_send.at[k], am_recv.at[k])
            got(b_meta.at[k], bm_send.at[k], bm_recv.at[k])
        copies = [
            pltpu.make_async_copy(a_meta.at[pl.ds(1, UNITS - 1)], a_idx.at[pl.ds(1, UNITS - 1)], idx_sem),
            pltpu.make_async_copy(b_meta.at[pl.ds(1, UNITS - 1)], b_idx.at[pl.ds(1, UNITS - 1)], b_idx_sem),
        ]
        for copy in copies:
            copy.start()
        for copy in copies:
            copy.wait()

    def b_unpack(u):
        way, core = (turn, q) if u < 4 else (-turn, 1 - q)
        group = (x + way * (0, -1, 1, -2)[u % 4] + 4) % 4

        def place(j, carry):
            slot = a_idx[0, SLOT, j] if u == 0 else b_idx[u, SLOT, j]
            flag = a_idx[0, FLAG, j] if u == 0 else b_idx[u, FLAG, j]
            b_dense[group, j, core] = split(b_units[u][slot] * flag.astype(jnp.float32))
            return carry

        lax.fori_loop(0, BAND, place, 0)

    def b_twin(u):
        send_b(4 + u, b_units[u], twin)

    def unit_row(t, way, core):
        step = jnp.where(t % 2 == 1, -((t + 1) // 2), t // 2)
        return 2 * ((z + way * step + 8) % 8) + core

    def roles(off):
        group = (x + off) % 4
        return group, (group - y + 4) % 4

    def weigh(t, load):
        for s in range(PER):
            part = split(load(s))
            weights[t, 2 * s * BS : (2 * s + 1) * BS, :] = part
            weights[t, (2 * s + 1) * BS : (2 * s + 2) * BS, :] = part

    def chunk(t, off):
        group, role = roles(off)
        i = unit_row(t, turn, q)
        places = [a_idx[t, LIST, s] for s in range(PER)]
        left = jnp.concatenate([b_dense[group, place].reshape(2 * BS, 2 * BS) for place in places], axis=1)
        both = jnp.dot(left, weights[t], preferred_element_type=jnp.float32)
        both = both[:, :BS] + both[:, BS:]
        partial[t, role, 0] = both[:BS]
        partial[t, role, 1] = both[BS:]

        @pl.when(role == 2)
        def _():
            for h, way in ((0, 1), (1, -1)):
                remote(
                    partial.at[t, 2, h], opposite.at[t, h], opp_send.at[t, h], opp_recv.at[t, h], ydev(way, q)
                ).start()

        @pl.when(role == 1)
        def _():
            remote(partial.at[t, 1, 1], from_left.at[i], un_send.at[t, 0], left_recv.at[i], ydev(1, 1)).start()

        @pl.when(role == 3)
        def _():
            remote(partial.at[t, 3, 0], from_right.at[i], un_send.at[t, 1], right_recv.at[i], ydev(-1, 0)).start()

        @pl.when(role == 0)
        def _():
            remote(partial.at[t, 0, 1 - q], from_twin.at[t], twin_send.at[t], twin_recv.at[t], twin).start()

    def merge(t, off):
        i = unit_row(t, turn, q)
        for h, mine, step, box, sem in ((0, 1, 1, from_left, left_recv), (1, 3, -1, from_right, right_recv)):
            @pl.when(roles(off)[1] == mine)
            def _():
                got(opposite.at[t, h], opp_send.at[t, h], opp_recv.at[t, h])
                merged[t, h] = opposite[t, h] + partial[t, mine, h]
                remote(merged.at[t, h], box.at[i], mg_send.at[t, h], sem.at[i], ydev(step, h)).start()

    def block_out(k):
        return out.at[pl.ds(pl.multiple_of(k * BS, BS), BS), :]

    def deliver(value, src, m, step, send):
        owner = 4 * ((x + step) % 4) + m

        @pl.when(owner == col)
        def _():
            block_out(col)[...] = value[...]

        @pl.when(owner != col)
        def _():
            remote(src, block_out(col), send, out_recv.at[col], at(col_=owner)).start()

    def relay(t, late):
        for core, way in ((q, turn), (1 - q, -turn)):
            i = unit_row(t, way, core)
            m = i // 4

            @pl.when((i % 4 == x) & (((x - y + 4) % 4 == 2) == late))
            def _():
                deliver(done.at[i], done.at[i], m, 0, done_send.at[i])

            for step in (1, 3, 2):
                @pl.when((i % 4 == x) & (((x + step - y + 4) % 4 == 2) == late))
                def _():
                    box = passing.at[m, step - 1]
                    got(box, done_send.at[i], pass_recv.at[m, step - 1])
                    deliver(box, box, m, step, pass_send.at[m, step - 1])

    def finish(t, late):
        @pl.when(((y - x + 4) % 4 == 2) == late)
        def _():
            finish_now(t)

    def finish_now(t):
        for core, way in ((q, turn), (1 - q, -turn)):
            i = unit_row(t, way, core)
            got(from_left.at[i], mg_send.at[0, 0], left_recv.at[i])
            got(from_right.at[i], mg_send.at[0, 0], right_recv.at[i])
            if core is q:
                own = partial[t, 0, q]
            else:
                got(from_twin.at[t], twin_send.at[t], twin_recv.at[t])
                own = from_twin[t]
            total = own + from_left[i] + from_right[i]
            done[i] = total
            m, step = i // 4, (x - i + 16) % 4

            @pl.when(step != 0)
            def _():
                remote(
                    done.at[i], passing.at[m, step - 1], done_send.at[i], pass_recv.at[m, step - 1], at(layer=i % 4)
                ).start()

    def each(first, stop, *steps):
        def body(t, carry):
            for step in steps:
                step(t)
            return carry

        lax.fori_loop(first, stop, body, 0)

    def chunks(*offs):
        return [functools.partial(chunk, off=off) for off in offs]

    def all_chunks(first, stop):
        def body(n, carry):
            chunk(n // 4, (n + 2) % 4)
            return carry

        lax.fori_loop(4 * first, 4 * stop, body, 0)

    def merges(*offs):
        return [functools.partial(merge, off=off) for off in offs]

    def finishes(late):
        return [functools.partial(finish, late=late)]

    def relays(late):
        return [functools.partial(relay, late=late)]

    def weigh_unit(t):
        weigh(t, lambda s: a_units[t, s])

    def pass_on(first, stop, part):
        each(
            first, stop, functools.partial(a_arrive, part=part), functools.partial(a_forward, part=part)
        )

    for part in range(2):
        send_a(1, part, packed, zdev(turn))
        send_a(2, part, packed, zdev(-turn))
    send_b(1, b_units[0], xdev(turn))
    send_b(2, b_units[0], xdev(-turn))
    indices()
    weigh(0, lambda s: packed[s])
    pass_on(1, 3, 0)
    b_twin(0)
    b_unpack(0)
    b_arrive(4)
    b_arrive(1)
    b_twin(1)
    send_b(3, b_units[1], xdev(turn))
    pass_on(1, 3, 1)
    b_arrive(2)
    b_unpack(4)
    each(1, 3, weigh_unit)
    chunk(0, 0)
    b_twin(2)
    b_unpack(2)
    b_unpack(1)
    each(1, 3, *chunks(0))
    b_arrive(6)
    b_unpack(6)
    b_arrive(5)
    b_unpack(5)
    each(0, 3, *chunks(1, 3))
    pass_on(3, 5, 0)
    each(1, 3, *merges(0))
    pass_on(3, 5, 1)
    merge(0, 0)
    each(0, 3, *merges(1, 3))
    b_arrive(3)
    b_twin(3)
    b_unpack(3)
    each(3, 5, weigh_unit)
    b_arrive(7)
    b_unpack(7)
    all_chunks(3, 5)
    pass_on(5, 6, 0)
    a_arrive(6, 0)
    each(0, 3, *finishes(False))
    a_arrive(6, 1)
    pass_on(5, 6, 1)
    each(3, 5, *merges(2))
    each(5, 7, weigh_unit)
    all_chunks(5, 7)
    each(3, 5, *merges(0, 1, 3))
    each(3, 5, *finishes(True))
    each(0, 3, *relays(False))
    a_arrive(7, 0)
    each(5, 7, *merges(0, 1, 3))
    a_arrive(7, 1)
    each(7, 8, weigh_unit)
    all_chunks(7, 8)
    each(5, 7, *merges(2))
    each(3, 5, *relays(True))
    each(3, 5, *finishes(False))
    each(0, 3, *chunks(2))
    each(5, 7, *finishes(False))
    each(5, 7, *finishes(True))
    each(7, 8, *merges(2))
    each(7, 8, *merges(0, 1, 3))
    each(3, 5, *relays(False))
    each(5, 7, *relays(True))
    each(0, 3, *merges(2))
    each(5, 7, *relays(False))
    each(7, 8, *finishes(False))
    each(7, 8, *finishes(True))
    each(7, 8, *relays(True))
    each(0, 3, *finishes(True))
    each(7, 8, *relays(False))
    each(0, 3, *relays(True))

    for k in range(1, UNITS):
        sent(a_meta.at[k], am_send.at[k], am_recv.at[k])
        for part in range(2):
            sent(part_of(a_units.at[k], part), a_send.at[k, part], a_recv.at[k, part])
        sent(b_meta.at[k], bm_send.at[k], bm_recv.at[k])
        sent(b_units[k], b_send.at[k], b_recv.at[k])

    def drain(t, carry):
        for h in range(2):
            sent(opposite.at[t, h], opp_send.at[t, h], opp_recv.at[t, h])
            sent(merged.at[t, h], mg_send.at[t, h], opp_recv.at[t, h])
            sent(merged.at[t, h], un_send.at[t, h], opp_recv.at[t, h])
        sent(from_twin.at[t], twin_send.at[t], twin_recv.at[t])
        return carry

    lax.fori_loop(0, UNITS, drain, 0)

    def collect(k, carry):
        @pl.when((k % 4 != x) | (4 * x + k // 4 != col))
        def _():
            sent(done.at[k], done_send.at[k], out_recv.at[k])

        @pl.when(k != col)
        def _():
            got(block_out(k), done_send.at[k], out_recv.at[k])

        for step in (1, 2, 3):
            @pl.when((k < 4) & (4 * ((x + step) % 4) + k != col))
            def _():
                m = lax.rem(k, 4)
                sent(passing.at[m, step - 1], pass_send.at[m, step - 1], out_recv.at[k])

        return carry

    lax.fori_loop(0, BAND, collect, 0)


def shards(matrix, pattern):
    f32, i32 = jnp.float32, jnp.int32
    dma = pltpu.SemaphoreType.DMA
    return pl.pallas_call(
        kernel,
        out_shape=jax.ShapeDtypeStruct(matrix.shape, f32),
        in_specs=[
            pl.BlockSpec(memory_space=pl.ANY),
            pl.BlockSpec(memory_space=pl.ANY),
        ],
        out_specs=pl.BlockSpec(memory_space=pltpu.VMEM),
        scratch_shapes=[
            pltpu.VMEM((BAND, BS, BS), f32),
            pltpu.SMEM((1, BAND), i32),
            pltpu.VMEM((8, 128), i32),
            pltpu.VMEM((PER, BS, BS), f32),
            pltpu.VMEM((UNITS, PER, BS, BS), f32),
            pltpu.VMEM((UNITS, 8, 128), i32),
            pltpu.SMEM((UNITS, 8, 128), i32),
            pltpu.VMEM((UNITS, 8, 128), i32),
            pltpu.SMEM((UNITS, 8, 128), i32),
            pltpu.VMEM((4, BAND, 2, BS, 2 * BS), jnp.bfloat16),
            pltpu.VMEM((UNITS, PER * 2 * BS, 2 * BS), jnp.bfloat16),
            pltpu.VMEM((UNITS, 4, 2, BS, BS), f32),
            pltpu.VMEM((UNITS, 2, BS, BS), f32),
            pltpu.VMEM((UNITS, 2, BS, BS), f32),
            pltpu.VMEM((BAND, BS, BS), f32),
            pltpu.VMEM((BAND, BS, BS), f32),
            pltpu.VMEM((UNITS, BS, BS), f32),
            pltpu.VMEM((BAND, BS, BS), f32),
            pltpu.VMEM((4, 3, BS, BS), f32),
        ]
        + [dma((UNITS, 2))] * 2
        + [dma((UNITS,))] * 6
        + [dma] * 2
        + [dma((UNITS, 2))] * 4
        + [dma((BAND,))] * 2
        + [dma((UNITS,))] * 2
        + [dma((BAND,)), dma((4, 3)), dma((4, 3)), dma((BAND,)), dma]
        + [pltpu.VMEM((PER, BS, BS), f32)] * UNITS,
        compiler_params=pltpu.CompilerParams(
            collective_id=0, has_side_effects=True, vmem_limit_bytes=52 * 1024 * 1024
        ),
    )(pattern.reshape(1, BAND), matrix.reshape(BAND, BS, BS))


def solution(mesh):
    return jax.shard_map(
        shards,
        mesh=mesh,
        in_specs=(P("row", ("layer", "col")), P("row", ("layer", "col"))),
        out_specs=P("row", ("col", "layer")),
        check_vma=False,
    )
```

```python
import functools

import jax
import jax.numpy as jnp
from jax import lax
from jax.experimental import pallas as pl
from jax.experimental.pallas import tpu as pltpu
from jax.sharding import PartitionSpec as P

BS = 128
PER = 7
BAND = 16
UNITS = 8
PARTS = ((0, 4), (4, 3))
LIST, SLOT, FLAG = 0, 1, 2


def index_lists(flags):
    counts, count = [], 0
    for flag in flags:
        count = count + flag
        counts.append(count)
    listed = [jnp.minimum(sum((c <= s).astype(jnp.int32) for c in counts), BAND - 1) for s in range(PER)]
    return listed, [jnp.clip(c - 1, 0, PER - 1) for c in counts]


def split(value):
    high = value.astype(jnp.bfloat16)
    low = (value - high.astype(jnp.float32)).astype(jnp.bfloat16)
    return jnp.concatenate([high, low], axis=1)


def kernel(
    pattern, matrix, out,
    mat, own, meta_v, packed, a_units, a_meta, a_idx, b_meta, b_idx, b_dense, weights,
    partial, merged, opposite, from_left, from_right, from_twin, done, passing,
    a_send, a_recv, am_send, am_recv, b_send, b_recv, bm_send, bm_recv, idx_sem, b_idx_sem,
    opp_send, opp_recv, mg_send, un_send, left_recv, right_recv, twin_send, twin_recv,
    done_send, pass_send, pass_recv, out_recv, mat_sem,
    *b_units,
):
    load = pltpu.make_async_copy(matrix, mat, mat_sem)
    load.start()
    flag_load = pltpu.make_async_copy(pattern, own, idx_sem)
    flag_load.start()
    y, col, x = lax.axis_index("row"), lax.axis_index("col"), lax.axis_index("layer")
    z, q = col // 2, col % 2
    turn = 1 - 2 * q

    def at(row=None, col_=None, layer=None):
        return {
            "row": y if row is None else row,
            "col": col if col_ is None else col_,
            "layer": x if layer is None else layer,
        }

    def zdev(step):
        return at(col_=2 * ((z + step + 8) % 8) + q)

    def xdev(step):
        return at(layer=(x + step + 4) % 4)

    def ydev(step, core):
        return at(row=(y + step + 4) % 4, col_=2 * z + core)

    twin = at(col_=2 * z + 1 - q)

    barrier = pltpu.get_barrier_semaphore()

    def greet(device):
        pl.semaphore_signal(barrier, inc=1, device_id=device, device_id_type=pl.DeviceIdType.MESH)

    for device in (ydev(1, 0), ydev(1, 1), ydev(-1, 0), ydev(-1, 1)):
        greet(device)
    for step in (1, 2, 3):
        greet(xdev(step))
        greet(at(col_=2 * z + 1 - q, layer=(x + step) % 4))

    def greet_line(k, carry):
        greet(at(col_=(col + k) % BAND))
        return carry

    lax.fori_loop(1, BAND, greet_line, 0)

    flag_load.wait()
    flags = [own[0, j] for j in range(BAND)]
    listed, slots = index_lists(flags)
    row, lane = (lax.broadcasted_iota(jnp.int32, (8, 128), d) for d in (0, 1))
    tile = jnp.zeros((8, 128), jnp.int32)
    for kind, values in ((LIST, listed), (SLOT, slots), (FLAG, flags)):
        for k, value in enumerate(values):
            tile = jnp.where((row == kind) & (lane == k), value, tile)
    meta_v[...] = tile
    load.wait()
    for s in range(PER):
        block = mat[listed[s]]
        packed[s] = block
    own_idx = pltpu.make_async_copy(meta_v, a_idx.at[0], idx_sem)
    own_idx.start()
    own_idx.wait()

    pl.semaphore_wait(barrier, 10 + BAND - 1)

    def remote(src, dst, send, recv, device):
        return pltpu.make_async_remote_copy(
            src_ref=src, dst_ref=dst, send_sem=send, recv_sem=recv,
            device_id=device, device_id_type=pl.DeviceIdType.MESH,
        )

    def got(dst, send, recv):
        remote(dst, dst, send, recv, twin).wait_recv()

    def sent(src, send, recv):
        remote(src, src, send, recv, twin).wait_send()

    def part_of(unit, part):
        return unit.at[pl.ds(*PARTS[part])]

    def send_a(t, part, data, device):
        remote(
            part_of(data, part), part_of(a_units.at[t], part), a_send.at[t, part], a_recv.at[t, part], device
        ).start()

    def send_b(u, data, device):
        remote(data, b_units[u], b_send.at[u], b_recv.at[u], device).start()

    def a_arrive(t, part):
        got(part_of(a_units.at[t], part), a_send.at[t, part], a_recv.at[t, part])

    def a_forward(t, part):
        way = jnp.where(t % 2 == 1, turn, -turn)
        send_a(t + 2, part, a_units.at[t], zdev(way))

    def b_arrive(u):
        got(b_units[u], b_send.at[u], b_recv.at[u])

    for t in range(1, UNITS):
        step = -((t + 1) // 2) if t % 2 else t // 2
        remote(meta_v, a_meta.at[t], am_send.at[t], am_recv.at[t], zdev(-turn * step)).start()
    for u in range(1, UNITS):
        step = (0, -1, 1, -2)[u % 4]
        device = at(col_=2 * z + (q if u < 4 else 1 - q), layer=(x - turn * step + 8) % 4)
        remote(meta_v, b_meta.at[u], bm_send.at[u], bm_recv.at[u], device).start()

    def indices():
        for k in range(1, UNITS):
            got(a_meta.at[k], am_send.at[k], am_recv.at[k])
            got(b_meta.at[k], bm_send.at[k], bm_recv.at[k])
        copies = [
            pltpu.make_async_copy(a_meta.at[pl.ds(1, UNITS - 1)], a_idx.at[pl.ds(1, UNITS - 1)], idx_sem),
            pltpu.make_async_copy(b_meta.at[pl.ds(1, UNITS - 1)], b_idx.at[pl.ds(1, UNITS - 1)], b_idx_sem),
        ]
        for copy in copies:
            copy.start()
        for copy in copies:
            copy.wait()

    def b_unpack(u):
        way, core = (turn, q) if u < 4 else (-turn, 1 - q)
        group = (x + way * (0, -1, 1, -2)[u % 4] + 4) % 4

        def place(j, carry):
            slot = a_idx[0, SLOT, j] if u == 0 else b_idx[u, SLOT, j]
            flag = a_idx[0, FLAG, j] if u == 0 else b_idx[u, FLAG, j]
            b_dense[group, j, core] = split(b_units[u][slot] * flag.astype(jnp.float32))
            return carry

        lax.fori_loop(0, BAND, place, 0)

    def b_twin(u):
        send_b(4 + u, b_units[u], twin)

    def unit_row(t, way, core):
        step = jnp.where(t % 2 == 1, -((t + 1) // 2), t // 2)
        return 2 * ((z + way * step + 8) % 8) + core

    def roles(off):
        group = (x + off) % 4
        return group, (group - y + 4) % 4

    def weigh(t, load):
        for s in range(PER):
            part = split(load(s))
            weights[t, 2 * s * BS : (2 * s + 1) * BS, :] = part
            weights[t, (2 * s + 1) * BS : (2 * s + 2) * BS, :] = part

    def chunk(t, off):
        group, role = roles(off)
        i = unit_row(t, turn, q)
        places = [a_idx[t, LIST, s] for s in range(PER)]
        left = jnp.concatenate([b_dense[group, place].reshape(2 * BS, 2 * BS) for place in places], axis=1)
        both = jnp.dot(left, weights[t], preferred_element_type=jnp.float32)
        both = both[:, :BS] + both[:, BS:]
        partial[t, role, 0] = both[:BS]
        partial[t, role, 1] = both[BS:]

        @pl.when(role == 2)
        def _():
            for h, way in ((0, 1), (1, -1)):
                remote(
                    partial.at[t, 2, h], opposite.at[t, h], opp_send.at[t, h], opp_recv.at[t, h], ydev(way, q)
                ).start()

        @pl.when(role == 1)
        def _():
            remote(partial.at[t, 1, 1], from_left.at[i], un_send.at[t, 0], left_recv.at[i], ydev(1, 1)).start()

        @pl.when(role == 3)
        def _():
            remote(partial.at[t, 3, 0], from_right.at[i], un_send.at[t, 1], right_recv.at[i], ydev(-1, 0)).start()

        @pl.when(role == 0)
        def _():
            remote(partial.at[t, 0, 1 - q], from_twin.at[t], twin_send.at[t], twin_recv.at[t], twin).start()

    def merge(t, off):
        i = unit_row(t, turn, q)
        for h, mine, step, box, sem in ((0, 1, 1, from_left, left_recv), (1, 3, -1, from_right, right_recv)):
            @pl.when(roles(off)[1] == mine)
            def _():
                got(opposite.at[t, h], opp_send.at[t, h], opp_recv.at[t, h])
                merged[t, h] = opposite[t, h] + partial[t, mine, h]
                remote(merged.at[t, h], box.at[i], mg_send.at[t, h], sem.at[i], ydev(step, h)).start()

    def block_out(k):
        return out.at[pl.ds(pl.multiple_of(k * BS, BS), BS), :]

    def deliver(value, src, m, step, send):
        owner = 4 * ((x + step) % 4) + m

        @pl.when(owner == col)
        def _():
            block_out(col)[...] = value[...]

        @pl.when(owner != col)
        def _():
            remote(src, block_out(col), send, out_recv.at[col], at(col_=owner)).start()

    def relay(t, late):
        for core, way in ((q, turn), (1 - q, -turn)):
            i = unit_row(t, way, core)
            m = i // 4

            @pl.when((i % 4 == x) & (((x - y + 4) % 4 == 2) == late))
            def _():
                deliver(done.at[i], done.at[i], m, 0, done_send.at[i])

            for step in (1, 3, 2):
                @pl.when((i % 4 == x) & (((x + step - y + 4) % 4 == 2) == late))
                def _():
                    box = passing.at[m, step - 1]
                    got(box, done_send.at[i], pass_recv.at[m, step - 1])
                    deliver(box, box, m, step, pass_send.at[m, step - 1])

    def finish(t, late):
        @pl.when(((y - x + 4) % 4 == 2) == late)
        def _():
            finish_now(t)

    def finish_now(t):
        for core, way in ((q, turn), (1 - q, -turn)):
            i = unit_row(t, way, core)
            got(from_left.at[i], mg_send.at[0, 0], left_recv.at[i])
            got(from_right.at[i], mg_send.at[0, 0], right_recv.at[i])
            if core is q:
                own = partial[t, 0, q]
            else:
                got(from_twin.at[t], twin_send.at[t], twin_recv.at[t])
                own = from_twin[t]
            total = own + from_left[i] + from_right[i]
            done[i] = total
            m, step = i // 4, (x - i + 16) % 4

            @pl.when(step != 0)
            def _():
                remote(
                    done.at[i], passing.at[m, step - 1], done_send.at[i], pass_recv.at[m, step - 1], at(layer=i % 4)
                ).start()

    def each(first, stop, *steps):
        def body(t, carry):
            for step in steps:
                step(t)
            return carry

        lax.fori_loop(first, stop, body, 0)

    def chunks(*offs):
        return [functools.partial(chunk, off=off) for off in offs]

    def all_chunks(first, stop):
        def body(n, carry):
            chunk(n // 4, (n + 2) % 4)
            return carry

        lax.fori_loop(4 * first, 4 * stop, body, 0)

    def merges(*offs):
        return [functools.partial(merge, off=off) for off in offs]

    def finishes(late):
        return [functools.partial(finish, late=late)]

    def relays(late):
        return [functools.partial(relay, late=late)]

    def weigh_unit(t):
        weigh(t, lambda s: a_units[t, s])

    def pass_on(first, stop, part):
        each(
            first, stop, functools.partial(a_arrive, part=part), functools.partial(a_forward, part=part)
        )

    for part in range(2):
        send_a(1, part, packed, zdev(turn))
        send_a(2, part, packed, zdev(-turn))
    for s in range(PER):
        b_units[0][s] = packed[s].T
    send_b(1, b_units[0], xdev(turn))
    send_b(2, b_units[0], xdev(-turn))
    indices()
    weigh(0, lambda s: packed[s])
    pass_on(1, 3, 0)
    b_twin(0)
    b_unpack(0)
    b_arrive(4)
    b_arrive(1)
    b_twin(1)
    send_b(3, b_units[1], xdev(turn))
    pass_on(1, 3, 1)
    b_arrive(2)
    b_unpack(4)
    each(1, 3, weigh_unit)
    chunk(0, 0)
    b_twin(2)
    b_unpack(2)
    b_unpack(1)
    each(1, 3, *chunks(0))
    b_arrive(6)
    b_unpack(6)
    b_arrive(5)
    b_unpack(5)
    each(0, 3, *chunks(1, 3))
    pass_on(3, 5, 0)
    each(1, 3, *merges(0))
    pass_on(3, 5, 1)
    merge(0, 0)
    each(0, 3, *merges(1, 3))
    b_arrive(3)
    b_twin(3)
    b_unpack(3)
    each(3, 5, weigh_unit)
    b_arrive(7)
    b_unpack(7)
    all_chunks(3, 5)
    pass_on(5, 6, 0)
    a_arrive(6, 0)
    each(0, 3, *finishes(False))
    a_arrive(6, 1)
    pass_on(5, 6, 1)
    each(3, 5, *merges(2))
    each(5, 7, weigh_unit)
    all_chunks(5, 7)
    each(3, 5, *merges(0, 1, 3))
    each(3, 5, *finishes(True))
    each(0, 3, *relays(False))
    a_arrive(7, 0)
    each(5, 7, *merges(0, 1, 3))
    a_arrive(7, 1)
    each(7, 8, weigh_unit)
    all_chunks(7, 8)
    each(5, 7, *merges(2))
    each(3, 5, *relays(True))
    each(3, 5, *finishes(False))
    each(0, 3, *chunks(2))
    each(5, 7, *finishes(False))
    each(5, 7, *finishes(True))
    each(7, 8, *merges(2))
    each(7, 8, *merges(0, 1, 3))
    each(3, 5, *relays(False))
    each(5, 7, *relays(True))
    each(0, 3, *merges(2))
    each(5, 7, *relays(False))
    each(7, 8, *finishes(False))
    each(7, 8, *finishes(True))
    each(7, 8, *relays(True))
    each(0, 3, *finishes(True))
    each(7, 8, *relays(False))
    each(0, 3, *relays(True))

    for k in range(1, UNITS):
        sent(a_meta.at[k], am_send.at[k], am_recv.at[k])
        for part in range(2):
            sent(part_of(a_units.at[k], part), a_send.at[k, part], a_recv.at[k, part])
        sent(b_meta.at[k], bm_send.at[k], bm_recv.at[k])
        sent(b_units[k], b_send.at[k], b_recv.at[k])

    def drain(t, carry):
        for h in range(2):
            sent(opposite.at[t, h], opp_send.at[t, h], opp_recv.at[t, h])
            sent(merged.at[t, h], mg_send.at[t, h], opp_recv.at[t, h])
            sent(merged.at[t, h], un_send.at[t, h], opp_recv.at[t, h])
        sent(from_twin.at[t], twin_send.at[t], twin_recv.at[t])
        return carry

    lax.fori_loop(0, UNITS, drain, 0)

    def collect(k, carry):
        @pl.when((k % 4 != x) | (4 * x + k // 4 != col))
        def _():
            sent(done.at[k], done_send.at[k], out_recv.at[k])

        @pl.when(k != col)
        def _():
            got(block_out(k), done_send.at[k], out_recv.at[k])

        for step in (1, 2, 3):
            @pl.when((k < 4) & (4 * ((x + step) % 4) + k != col))
            def _():
                m = lax.rem(k, 4)
                sent(passing.at[m, step - 1], pass_send.at[m, step - 1], out_recv.at[k])

        return carry

    lax.fori_loop(0, BAND, collect, 0)


def shards(matrix, pattern):
    f32, i32 = jnp.float32, jnp.int32
    dma = pltpu.SemaphoreType.DMA
    return pl.pallas_call(
        kernel,
        out_shape=jax.ShapeDtypeStruct(matrix.shape, f32),
        in_specs=[
            pl.BlockSpec(memory_space=pl.ANY),
            pl.BlockSpec(memory_space=pl.ANY),
        ],
        out_specs=pl.BlockSpec(memory_space=pltpu.VMEM),
        scratch_shapes=[
            pltpu.VMEM((BAND, BS, BS), f32),
            pltpu.SMEM((1, BAND), i32),
            pltpu.VMEM((8, 128), i32),
            pltpu.VMEM((PER, BS, BS), f32),
            pltpu.VMEM((UNITS, PER, BS, BS), f32),
            pltpu.VMEM((UNITS, 8, 128), i32),
            pltpu.SMEM((UNITS, 8, 128), i32),
            pltpu.VMEM((UNITS, 8, 128), i32),
            pltpu.SMEM((UNITS, 8, 128), i32),
            pltpu.VMEM((4, BAND, 2, BS, 2 * BS), jnp.bfloat16),
            pltpu.VMEM((UNITS, PER * 2 * BS, 2 * BS), jnp.bfloat16),
            pltpu.VMEM((UNITS, 4, 2, BS, BS), f32),
            pltpu.VMEM((UNITS, 2, BS, BS), f32),
            pltpu.VMEM((UNITS, 2, BS, BS), f32),
            pltpu.VMEM((BAND, BS, BS), f32),
            pltpu.VMEM((BAND, BS, BS), f32),
            pltpu.VMEM((UNITS, BS, BS), f32),
            pltpu.VMEM((BAND, BS, BS), f32),
            pltpu.VMEM((4, 3, BS, BS), f32),
        ]
        + [dma((UNITS, 2))] * 2
        + [dma((UNITS,))] * 6
        + [dma] * 2
        + [dma((UNITS, 2))] * 4
        + [dma((BAND,))] * 2
        + [dma((UNITS,))] * 2
        + [dma((BAND,)), dma((4, 3)), dma((4, 3)), dma((BAND,)), dma]
        + [pltpu.VMEM((PER, BS, BS), f32)] * UNITS,
        compiler_params=pltpu.CompilerParams(
            collective_id=0, has_side_effects=True, vmem_limit_bytes=52 * 1024 * 1024
        ),
    )(pattern.reshape(1, BAND), matrix.reshape(BAND, BS, BS))


def solution(mesh):
    return jax.shard_map(
        shards,
        mesh=mesh,
        in_specs=(P("row", ("layer", "col")), P("row", ("layer", "col"))),
        out_specs=P("row", ("col", "layer")),
        check_vma=False,
    )
```
